256 devices in a mesh: frm: 32 (over z_hi, x, core), head: 8 (over z_lo, y).
Axes of the slice: x: 4, y: 4, z: 8 (z_hi: 4, z_lo: 2; z = z_hi * 2 + z_lo), core: 2. Of those that a mesh axis runs over, the one named last changes fastest.
Arguments:
- video_q: bfloat16 [8192, 3072], P('frm', 'head'), may hold values from -8 to 8
- video_k: bfloat16 [8192, 3072], P('frm', 'head'), may hold values from -8 to 8
- video_v: bfloat16 [8192, 3072], P('frm', 'head'), may hold values from -6 to 6
- text_q: bfloat16 [256, 3072], P(None, 'head'), may hold values from -8 to 8
- text_k: bfloat16 [256, 3072], P(None, 'head'), may hold values from -8 to 8
- text_v: bfloat16 [256, 3072], P(None, 'head'), may hold values from -6 to 6
- band_start: int32 [32], P('frm'), may hold values from 0 to 1, as said below
- text_mask: int32 [256], replicated, may hold values 0 or 1
- video_proj: bfloat16 [3072, 3072], P('head'), may hold values from -0.109375 to 0.109375
- text_proj: bfloat16 [3072, 3072], P('head'), may hold values from -0.109375 to 0.109375
Outputs:
- video_out: float32 [8192, 3072], P(('frm', 'head'))
- text_out: float32 [256, 3072], P('head')
The draws below stay inside these ranges and needn't reach their ends.
Inputs may be any that keep to these rules, and one draw needn't show every extreme that they name: `band_start`: the window of 3 bands of every query tile contains the tile's own band.
All inputs are finite; a program needn't handle non-finite values.
Results may differ from the reference program's by a relative error of at most 0.009.
Values may be sent and summed in bfloat16 or wider, within the bound.
A program may use at most 128 MiB of HBM per device.

```python
import math
import jax
import jax.numpy as jnp
from jax import lax

D = 3072
HEADS = 24
HD = 128
TXT = 256
BANDS = 4
BAND_WIN = 3
TILE = 256
TILES = 32
VID = 8192


def normal_rows(key, count, spread):
    return jnp.clip(spread * jax.random.normal(key, (count, HEADS * HD), jnp.float32), -8.0, 8.0)


def draw_video_q(key, part):
    key = jax.random.fold_in(key, 101)
    values = normal_rows(key, VID, 1.4)
    return values.astype(jnp.bfloat16)


def draw_video_k(key, part):
    key = jax.random.fold_in(key, 202)
    values = normal_rows(key, VID, 1.4)
    return values.astype(jnp.bfloat16)


def draw_text_q(key, part):
    key = jax.random.fold_in(key, 303)
    values = normal_rows(key, TXT, 1.4)
    return values.astype(jnp.bfloat16)


def draw_text_k(key, part):
    key = jax.random.fold_in(key, 404)
    values = normal_rows(key, TXT, 1.4)
    return values.astype(jnp.bfloat16)


def draw_band_start(key, part):
    key = jax.random.fold_in(key, 91)
    own_bands = jnp.arange(TILES, dtype=jnp.int32) % BANDS
    coin_flip = jax.random.randint(key, (TILES,), 0, BANDS - BAND_WIN + 1, dtype=jnp.int32)
    lowest = jnp.maximum(own_bands - (BAND_WIN - 1), 0)
    highest = jnp.minimum(own_bands, BANDS - BAND_WIN)
    return jnp.clip(coin_flip, lowest, highest).astype(jnp.int32)


def with_ends(values, stream_key, least, top_value):
    index_at = [jax.random.randint(jax.random.fold_in(stream_key, axis), (), 0, length) for axis, length in enumerate(values.shape)]
    longest = values.shape.index(max(values.shape))
    beside = index_at[:longest] + [(index_at[longest] + 1) % values.shape[longest]] + index_at[longest + 1:]
    return values.at[tuple(index_at)].set(least).at[tuple(beside)].set(top_value)


def shard_levels(own_key, dims, shards, smallest, high):
    factor_of, own = 1.0, jax.random.fold_in(own_key, 6)
    for axis_at, blocks in shards:
        steps = jnp.exp(jax.random.uniform(jax.random.fold_in(own, axis_at), (blocks,), jnp.float32, smallest / len(shards), high / len(shards)))
        factor_of = factor_of * jnp.repeat(steps, dims[axis_at] // blocks).reshape([-1 if axis == axis_at else 1 for axis in range(len(dims))])
    return factor_of


def normal_values(key, dims, deviation, limit, shards=(), held_as=jnp.bfloat16):
    array = jax.random.normal(key, dims, jnp.float32) * deviation
    if len(shards) > 0:
        array = shard_levels(key, dims, shards, -0.22, 0.18) * array
    return jnp.clip(array, min=-limit, max=limit).astype(held_as)


def setup_inputs(seed: int = 0) -> dict:
    splits = jax.random.split(jax.random.key(seed), 11)
    return {
        "video_q": draw_video_q(jax.random.fold_in(splits[10], 71), 0),
        "video_k": draw_video_k(jax.random.fold_in(splits[10], 71), 0),
        "video_v": normal_values(splits[2], (VID, HEADS * HD), 1.0, 6.0, ((0, 32), (1, 8))),
        "text_q": draw_text_q(jax.random.fold_in(splits[10], 71), 0),
        "text_k": draw_text_k(jax.random.fold_in(splits[10], 71), 0),
        "text_v": normal_values(splits[5], (TXT, HEADS * HD), 1.0, 6.0, ((1, 8),)),
        "band_start": draw_band_start(jax.random.fold_in(splits[10], 71), 0),
        "text_mask": with_ends((jax.random.randint(splits[7], (TXT,), 0, 4) < 3).astype(jnp.int32), jax.random.fold_in(splits[7], 1), 0, 1),
        "video_proj": normal_values(splits[8], (HEADS * HD, D), (HEADS * HD) ** -0.5, 0.109375, ((0, 8),)),
        "text_proj": normal_values(splits[9], (HEADS * HD, D), (HEADS * HD) ** -0.5, 0.109375, ((0, 8),)),
    }


def softmax_values(scores, values):
    row_max = lax.optimization_barrier(jnp.max(scores, axis=-1, keepdims=True))
    weights = jnp.exp(scores - row_max)
    row_total = lax.optimization_barrier(jnp.sum(weights, axis=-1))
    rounded = lax.optimization_barrier(weights.astype(jnp.bfloat16)).astype(jnp.float32)
    mixed_sum = jnp.einsum('hqk,khd->qhd', rounded, values.astype(jnp.float32))
    return mixed_sum / jnp.transpose(row_total)[:, :, None]

def reference(video_q, video_k, video_v, text_q, text_k, text_v, band_start, text_mask, video_proj, text_proj):
    scale = 1.0 / math.sqrt(HD)
    frame_count = TILES // BANDS
    zero_frame = jnp.zeros((1, BANDS, TILE, HEADS, HD), jnp.bfloat16)
    key_pad = jnp.concatenate([zero_frame, video_k.reshape(frame_count, BANDS, TILE, HEADS, HD), zero_frame], 0)
    value_pad = jnp.concatenate([zero_frame, video_v.reshape(frame_count, BANDS, TILE, HEADS, HD), zero_frame], 0)
    text_keys = text_k.reshape(TXT, HEADS, HD)
    text_values = text_v.reshape(TXT, HEADS, HD)
    text_valid = text_mask == 1

    def one_tile(tile_index):
        frame_index = tile_index // BANDS
        first_band = band_start[tile_index]
        queries = lax.dynamic_slice_in_dim(video_q, tile_index * TILE, TILE, 0).reshape(TILE, HEADS, HD).astype(jnp.float32)
        anchor = (frame_index, first_band, jnp.int32(0), jnp.int32(0), jnp.int32(0))
        key_block = lax.dynamic_slice(key_pad, anchor, (3, BAND_WIN, TILE, HEADS, HD)).reshape(3 * BAND_WIN * TILE, HEADS, HD)
        value_block = lax.dynamic_slice(value_pad, anchor, (3, BAND_WIN, TILE, HEADS, HD)).reshape(3 * BAND_WIN * TILE, HEADS, HD)
        near_frames = frame_index + jnp.arange(3, dtype=jnp.int32) - 1
        inside = (near_frames >= 0) & (near_frames < frame_count)
        live_keys = jnp.concatenate([jnp.repeat(inside, BAND_WIN * TILE), text_valid])
        all_keys = jnp.concatenate([key_block, text_keys], 0).astype(jnp.float32)
        all_values = jnp.concatenate([value_block, text_values], 0)
        scores = jnp.einsum('qhd,khd->hqk', queries, all_keys) * scale
        scores = jnp.where(live_keys[None, None, :], scores, -jnp.inf)
        return softmax_values(scores, all_values).reshape(TILE, HEADS * HD).astype(jnp.bfloat16)
    video_attn = lax.map(one_tile, jnp.arange(TILES, dtype=jnp.int32)).reshape(TILES * TILE, HEADS * HD)
    every_key = jnp.concatenate([video_k, text_k], 0)
    every_value = jnp.concatenate([video_v, text_v], 0)
    text_live = jnp.concatenate([jnp.ones((VID,), bool), text_valid])

    def one_head(head_index):
        head_queries = lax.dynamic_slice_in_dim(text_q, head_index * HD, HD, 1)
        head_keys = lax.dynamic_slice_in_dim(every_key, head_index * HD, HD, 1)
        head_values = lax.dynamic_slice_in_dim(every_value, head_index * HD, HD, 1)
        scores = jnp.dot(head_queries, jnp.transpose(head_keys), preferred_element_type=jnp.float32) * scale
        scores = jnp.where(text_live[None, :], scores, -jnp.inf)
        row_max = lax.optimization_barrier(jnp.max(scores, axis=-1, keepdims=True))
        weights = jnp.exp(scores - row_max)
        row_total = lax.optimization_barrier(jnp.sum(weights, axis=-1))
        mixed_sum = jnp.dot(weights.astype(jnp.bfloat16), head_values, preferred_element_type=jnp.float32)
        return (mixed_sum / row_total[:, None]).astype(jnp.bfloat16)
    per_head = lax.map(one_head, jnp.arange(HEADS, dtype=jnp.int32))
    text_attn = jnp.transpose(per_head, (1, 0, 2)).reshape(TXT, HEADS * HD)
    video_out = jnp.dot(video_attn, video_proj, preferred_element_type=jnp.float32)
    text_out = jnp.dot(text_attn, text_proj, preferred_element_type=jnp.float32)
    return (video_out, text_out)
```

```python
import math

import jax
import jax.numpy as jnp
from jax import lax
from jax.experimental import pallas as pl
from jax.experimental.pallas import tpu as pltpu
from jax.sharding import PartitionSpec as P

HD = 128
TXT = 256
BANDS = 4
HEADS_HERE = 3
LANES = HEADS_HERE * HD
WIDTH = 3072
MESH = pl.DeviceIdType.MESH
BF = jnp.bfloat16
F32 = jnp.float32
FACTOR = math.log2(math.e) / math.sqrt(HD)
DEAD = -1e30
CHUNKS = 2
OWN, MATE, OPP, INTER, VMATE, VERT = range(6)
Z_FIRST = ((0, 1024),)
Y_FIRST = ((1024, 1024), (2048, 1024))
BLOCK = 512


def dot_nt(a, b):
    return lax.dot_general(a, b, (((1,), (1,)), ((), ())), preferred_element_type=F32)


def dot_nn(a, b):
    return jnp.dot(a, b, preferred_element_type=F32)


def with_ones(values):
    return jnp.concatenate([values, jnp.ones(values.shape, BF)], axis=1)


def kernel(
    vq_hbm, vk_hbm, vv_hbm, tq_hbm, tk_hbm, tv_hbm, band_ref, mask_ref, vproj_hbm, tproj_hbm,
    vout_ref, tout_ref,
    kv_a, kv_b, kv_c, vq, tq, tk, tv, vproj, tproj, state_o, state_m, attn, part,
    kv_send, kv_recv, load_sem,
    t_a, t_ar, t_b, t_br, t_c, t_cr, t_z, t_zr, t_rows, t_sums, t_sumr, t_out,
    ta_sem, tz_send, tz_recv, tg_send, tg_recv, ts_send, ts_recv, to_send, to_recv,
    zf_in, zf_sum, r1, r2, stage, zs, zr,
    zf_sem, r_send, r_recv, zx_sem,
):
    frm = lax.axis_index("frm")
    head = lax.axis_index("head")
    zh, x, c = frm // 8, (frm // 2) % 4, frm % 2
    zl, y = head // 4, head % 4
    xr, xo = x // 2, x % 2

    def at(zh_, x_, c_):
        return {"frm": zh_ * 8 + x_ * 2 + c_, "head": head}

    def at_head(zl_, y_):
        return {"frm": frm, "head": zl_ * 4 + y_}

    x_mate = x + 1 - 2 * xo
    sib = at(zh, x, 1 - c)
    mate = at(zh, x_mate, c)
    inter = at(zh, 3 - x, c)
    z_pair = at_head(1 - zl, y)
    yp, ym, yo = (y + 1) % 4, (y + 3) % 4, (y + 2) % 4
    zh_to = zh + 1 - 2 * xr
    v_send = (zh_to >= 0) & (zh_to <= 3)
    zh_from = zh - 1 + 2 * xr
    v_recv = (zh_from >= 0) & (zh_from <= 3)
    vert = at(jnp.clip(zh_to, 0, 3), x, c)

    def copy_to(src, dst, send, recv, device):
        return pltpu.make_async_remote_copy(
            src_ref=src, dst_ref=dst, send_sem=send, recv_sem=recv,
            device_id=device, device_id_type=MESH,
        )

    loads = []

    def load(src, dst):
        copy = pltpu.make_async_copy(src, dst, load_sem.at[len(loads)])
        copy.start()
        loads.append(copy)
        return copy

    load_own = [load(vk_hbm, kv_a.at[0, 0]), load(vv_hbm, kv_a.at[0, 1])]
    load_text = [load(tq_hbm, tq), load(tk_hbm, tk), load(tv_hbm, tv)]
    load_q = load(vq_hbm, vq)
    load_vproj = load(vproj_hbm, vproj)
    piece = 2 * x + zh // 2
    load_tproj = load(tproj_hbm.at[:, pl.ds(pl.multiple_of(piece * LANES, LANES), LANES)], tproj)

    frm_partners = [sib]
    for dz in range(4):
        for dx in range(4):
            if (dz, dx) != (0, 0) and (dz % 2 == 0 or dx == 0):
                frm_partners.append(at((zh + dz) % 4, (x + dx) % 4, c))
    gather_partners = [
        at((zh + dz) % 4, (x + dx) % 4, c)
        for dz in (0, 2) for dx in range(4) if (dz, dx) != (0, 0)
    ]
    head_partners = [
        ((zl + dz) % 2, (y + dy) % 4) for dz in range(2) for dy in range(4) if (dz, dy) != (0, 0)
    ]
    barrier = pltpu.get_barrier_semaphore()
    for device in frm_partners + [at_head(a, b) for a, b in head_partners]:
        pl.semaphore_signal(barrier, inc=1, device_id=device, device_id_type=MESH)
    pl.semaphore_wait(barrier, len(frm_partners) + len(head_partners))

    rows = 256 // CHUNKS
    sends = []

    def kv_copy(kind, t, j, src_slot, dst_slot, device, src=None):
        rng = pl.ds(j * rows, rows)
        return copy_to(
            kv_of[src_slot // 4].at[src_slot % 4, t, rng] if src is None else src.at[rng],
            kv_of[dst_slot // 4].at[dst_slot % 4, t, rng],
            kv_send.at[kind, t, j],
            kv_recv.at[dst_slot, t, j],
            device,
        )

    kv_of = (kv_a, kv_b, kv_c)
    pieces = [(t, j) for t in range(2) for j in range(CHUNKS)]
    own_hbm = (vk_hbm, vv_hbm)

    def to_mate(t, j):
        return kv_copy(0, t, j, 0, 2 * MATE, mate, own_hbm[t])

    def to_inter(t, j):
        return kv_copy(1, t, j, 0, 2 * INTER, inter, own_hbm[t])

    def to_opp(t, j):
        if t == 0:
            return kv_copy(2, t, j, 2 * INTER, 2 * OPP, mate)
        return kv_copy(2, t, j, 2 * MATE, 2 * OPP, inter)

    def to_vert(t, j):
        return kv_copy(3, t, j, 2 * INTER, 2 * VERT, vert)

    def to_vmate(t, j):
        return kv_copy(4, t, j, 2 * VERT, 2 * VMATE, mate)

    def to_sib(role, t, j):
        return kv_copy(5 + role, t, j, 2 * role, 2 * role + 1, sib, own_hbm[t] if role == OWN else None)

    def go(copy):
        copy.start()
        sends.append(copy)

    for t, j in pieces:
        go(to_inter(t, j))
        go(to_mate(t, j))
    for t, j in pieces:
        go(to_sib(OWN, t, j))

    for copy in load_own + load_text:
        copy.wait()
    lane = lax.broadcasted_iota(jnp.int32, (1, TXT), 1)
    text_bias = jnp.where(mask_ref[...] == 1, 0.0, DEAD)
    first_bias = jnp.where(frm == 0, text_bias, DEAD)

    def pack_stats(tops, totals):
        count = tops[0].shape[0]
        at_lane = lax.broadcasted_iota(jnp.int32, (count, HD), 1)
        packed = jnp.zeros((count, HD), F32)
        for h in range(HEADS_HERE):
            high = totals[h].astype(BF).astype(F32)
            packed = jnp.where(at_lane == h, tops[h], packed)
            packed = jnp.where(at_lane == 3 + h, high, packed)
            packed = jnp.where(at_lane == 6 + h, totals[h] - high, packed)
        return packed

    tops, totals, mixed = [], [], []
    for h in range(HEADS_HERE):
        cols = slice(h * HD, (h + 1) * HD)
        s_own = dot_nt(tq[:, cols], kv_a[0, 0, :, cols])
        s_text = dot_nt(tq[:, cols], tk[:, cols]) + first_bias
        top = jnp.maximum(
            jnp.max(s_own, axis=1, keepdims=True), jnp.max(s_text, axis=1, keepdims=True)
        ).astype(BF).astype(F32)
        base = top * FACTOR
        w_own = jnp.exp2(s_own * FACTOR - base).astype(BF)
        w_text = jnp.exp2(s_text * FACTOR - base).astype(BF)
        both = dot_nn(w_own, with_ones(kv_a[0, 1, :, cols])) + dot_nn(w_text, with_ones(tv[:, cols]))
        tops.append(top)
        totals.append(both[:, HD:HD + 1])
        mixed.append(both[:, :HD].astype(BF))
    stats = pack_stats(tops, totals).astype(BF)
    for h_to in range(8):
        for half in range(2):
            rng = slice(32 * h_to + 16 * half, 32 * h_to + 16 * half + 16)
            for h in range(HEADS_HERE):
                t_a[half, h_to, :, h * HD:(h + 1) * HD] = mixed[h][rng]
            t_a[half, h_to, :, LANES:] = stats[rng]

    text_a = copy_to(t_a.at[1 - c], t_ar, ta_sem.at[0], ta_sem.at[1], sib)
    go(text_a)

    def merge(parts):
        parts = [p.astype(F32) for p in parts]
        out_tops, out_totals, out_mixed = [], [], []
        for h in range(HEADS_HERE):
            tops_h = [p[:, LANES + h:LANES + h + 1] for p in parts]
            top = tops_h[0]
            for other in tops_h[1:]:
                top = jnp.maximum(top, other)
            total, mix = 0.0, 0.0
            for p, top_p in zip(parts, tops_h):
                weight = jnp.exp2((top_p - top) * FACTOR)
                total_p = p[:, LANES + 3 + h:LANES + 4 + h] + p[:, LANES + 6 + h:LANES + 7 + h]
                total = total + total_p * weight
                mix = mix + p[:, h * HD:(h + 1) * HD] * weight
            out_tops.append(top)
            out_totals.append(total)
            out_mixed.append(mix)
        return out_tops, out_totals, out_mixed

    def merged(parts):
        out_tops, out_totals, out_mixed = merge(parts)
        return jnp.concatenate(out_mixed + [pack_stats(out_tops, out_totals)], axis=1)

    def group(kv, fresh):
        mid = c != xo
        at_b = jnp.where(mid, 3, 1)
        pick_same = mid & (band_ref[0] == xo)
        at_c = jnp.where(pick_same, 1, 2)
        slots = (0, at_b, at_c)

        @pl.loop(0, HEADS_HERE)
        def _(h):
            cols = pl.ds(pl.multiple_of(h * HD, HD), HD)
            query = vq[:, cols]
            scores = [dot_nt(query, kv[s, 0, :, cols]) for s in slots]
            top = jnp.max(jnp.maximum(jnp.maximum(scores[0], scores[1]), scores[2]), axis=1, keepdims=True)
            if not fresh:
                old = state_m[h]
                top = jnp.maximum(top, old[:, :1])
            base = top * FACTOR
            total = None
            for s, score in zip(slots, scores):
                weights = jnp.exp2(score * FACTOR - base).astype(BF)
                term = dot_nn(weights, with_ones(kv[s, 1, :, cols]))
                total = term if total is None else total + term
            if not fresh:
                total = total + state_o[h] * jnp.exp2(old[:, :1] * FACTOR - base)
            state_o[h] = total
            state_m[h] = jnp.broadcast_to(top, (256, HD))

    def text_keys():
        @pl.loop(0, HEADS_HERE)
        def _(h):
            cols = pl.ds(pl.multiple_of(h * HD, HD), HD)
            score = dot_nt(vq[:, cols], tk[:, cols]) + text_bias
            old = state_m[h]
            top = jnp.maximum(jnp.max(score, axis=1, keepdims=True), old[:, :1])
            base = top * FACTOR
            weights = jnp.exp2(score * FACTOR - base).astype(BF)
            total = dot_nn(weights, with_ones(tv[:, cols]))
            state_o[h] = total + state_o[h] * jnp.exp2(old[:, :1] * FACTOR - base)
            state_m[h] = jnp.broadcast_to(top, (256, HD))

    def serve(t, j):
        to_inter(t, j).wait_recv()

        @pl.when(v_send)
        def _():
            to_vert(t, j).start()

        if t == 0:
            go(to_opp(t, j))
        go(to_sib(INTER, t, j))
        to_mate(t, j).wait_recv()
        if t == 1:
            go(to_opp(t, j))
        go(to_sib(MATE, t, j))

    def text_step_a():
        text_a.wait_recv()
        for h_to in range(8):
            t_b[h_to // 4, h_to % 4] = merged([t_a[c, h_to], t_ar[h_to]]).astype(BF)
        copy = copy_to(t_b.at[1 - xr], t_br, ta_sem.at[2], ta_sem.at[3], inter)
        go(copy)
        return copy

    def text_step_b(copy):
        copy.wait_recv()
        for k in range(4):
            t_c[k // 2, k % 2] = merged([t_b[xr, k], t_br[k]]).astype(BF)
        copy = copy_to(t_c.at[1 - xo], t_cr, ta_sem.at[4], ta_sem.at[5], mate)
        go(copy)
        return copy

    def text_step_c(copy):
        copy.wait_recv()
        for k in range(2):
            both = merged([t_c[xo, k], t_cr[k]])
            t_z[2 * k] = both[:8]
            t_z[2 * k + 1] = both[8:]
        copies = []
        for dz in range(1, 4):
            to = (zh + dz) % 4
            copy = copy_to(t_z.at[to], t_zr.at[dz], tz_send.at[dz], tz_recv.at[dz], at(to, x, c))
            go(copy)
            copies.append(copy)
        return copies

    def text_step_z(copies):
        for copy in copies:
            copy.wait_recv()
        _, sums, mix = merge([t_z[zh], t_zr[1], t_zr[2], t_zr[3]])
        for h in range(HEADS_HERE):
            t_rows[piece, :, h * HD:(h + 1) * HD] = (mix[h] / sums[h]).astype(BF).astype(F32)
        out = []
        for k, device in enumerate(gather_partners):
            copy = copy_to(t_rows.at[piece], t_rows.at[piece], tg_send.at[k], tg_recv.at[k], device)
            go(copy)
            out.append(copy)
        return out

    def text_gather(copies):
        k = 0
        for dz in (0, 2):
            for dx in range(4):
                if (dz, dx) == (0, 0):
                    continue
                source = 2 * ((x - dx + 4) % 4) + ((zh - dz + 4) % 4) // 2
                copy_to(
                    t_rows.at[source], t_rows.at[source], tg_send.at[k], tg_recv.at[k], sib
                ).wait_recv()
                k += 1
        load_tproj.wait()
        rows_all = jnp.concatenate([t_rows[k] for k in range(8)], axis=0).astype(BF)
        product = dot_nn(rows_all, tproj[...])
        for k in range(8):
            t_sums[k] = product[8 * k:8 * k + 8]
        out = []
        for k, (a, b) in enumerate(head_partners):
            copy = copy_to(t_sums.at[a * 4 + b], t_sumr.at[k], ts_send.at[k], ts_recv.at[k], at_head(a, b))
            go(copy)
            out.append(copy)
        return out

    def text_sum(copies):
        for copy in copies:
            copy.wait_recv()
        total = t_sums[head]
        for k in range(7):
            total = total + t_sumr[k]
        t_out[c, zh % 2, x, zh // 2] = total
        out = []
        for dz in range(1, 4):
            block = t_out.at[c, zh % 2, x, zh // 2]
            copy = copy_to(block, block, to_send.at[dz], to_recv.at[dz], at((zh + dz) % 4, x, c))
            go(copy)
            out.append(copy)
        return out

    def text_spread_mate():
        for dz in range(1, 4):
            source = (zh - dz + 4) % 4
            block = t_out.at[c, source % 2, x, source // 2]
            copy_to(block, block, to_send.at[dz], to_recv.at[dz], sib).wait_recv()
        block = t_out.at[c, :, x]
        go(copy_to(block, block, to_send.at[4], to_recv.at[4], mate))

    def text_spread_inter():
        block = t_out.at[c, :, x_mate]
        copy_to(block, block, to_send.at[4], to_recv.at[4], mate).wait_recv()
        block = t_out.at[c, :, pl.ds(2 * xr, 2)]
        go(copy_to(block, block, to_send.at[5], to_recv.at[5], inter))

    def text_spread_sib():
        block = t_out.at[c, :, pl.ds(2 - 2 * xr, 2)]
        copy_to(block, block, to_send.at[5], to_recv.at[5], inter).wait_recv()
        go(copy_to(t_out.at[c], t_out.at[c], to_send.at[6], to_recv.at[6], sib))

    def text_finish():
        block = t_out.at[1 - c]
        copy_to(block, block, to_send.at[6], to_recv.at[6], sib).wait_recv()
        for cc in range(2):
            for q in range(2):
                for k in range(8):
                    tout_ref[16 * cc + 8 * q:16 * cc + 8 * q + 8, k * LANES:(k + 1) * LANES] = (
                        t_out[cc, q, k // 2, k % 2]
                    )

    serve(*pieces[0])
    text_copy = text_step_a()
    serve(*pieces[1])
    text_copy = text_step_b(text_copy)
    for p in pieces[2:]:
        serve(*p)
    text_copies = text_step_c(text_copy)

    load_q.wait()
    for role in (OWN, MATE):
        for t, j in pieces:
            to_sib(role, t, j).wait_recv()
    group(kv_a, True)

    text_copies = text_step_z(text_copies)

    def serve_vert(t, j):
        @pl.when(v_recv)
        def _():
            to_vert(t, j).wait_recv()
            to_vmate(t, j).start()
            to_sib(VERT, t, j).start()

    serve_vert(*pieces[0])
    for t, j in pieces:
        to_opp(t, j).wait_recv()
        go(to_sib(OPP, t, j))
    text_keys()
    serve_vert(*pieces[1])

    for role in (OPP, INTER):
        for t, j in pieces:
            to_sib(role, t, j).wait_recv()
    group(kv_b, False)
    serve_vert(*pieces[2])
    text_copies = text_gather(text_copies)

    for p in pieces[3:]:
        serve_vert(*p)

    @pl.when(v_recv)
    def _():
        for t, j in pieces:
            to_vmate(t, j).wait_recv()
            to_sib(VMATE, t, j).start()
        for role in (VERT, VMATE):
            for t, j in pieces:
                to_sib(role, t, j).wait_recv()
        group(kv_c, False)

    for h in range(HEADS_HERE):
        both = state_o[h]
        attn[:, h * HD:(h + 1) * HD] = (both[:, :HD] / both[:, HD:]).astype(BF)
    load_vproj.wait()

    def project(start, width):
        @pl.loop(0, width // BLOCK)
        def _(i):
            cols = pl.ds(pl.multiple_of(start + i * BLOCK, BLOCK), BLOCK)
            product = dot_nn(attn[...], vproj[:, cols]).astype(BF)
            for k in range(8):
                part[k // 4, k % 4, :, cols] = product[32 * k:32 * k + 32]

    zf_copies = []
    for i, (start, width) in enumerate(Z_FIRST):
        project(start, width)
        copy = copy_to(
            part.at[1 - zl, :, :, pl.ds(start, width)], zf_in.at[i], zf_sem.at[0, i], zf_sem.at[1, i], z_pair
        )
        go(copy)
        zf_copies.append(copy)

    y_next, y_prev = at_head(zl, yp), at_head(zl, ym)

    def ring_start(i, block, half):
        one = [
            copy_to(block(yo, 0), r1.at[i, 0], r_send.at[i, 0], r_recv.at[i, 0], y_next),
            copy_to(block(yo, half), r1.at[i, 1], r_send.at[i, 1], r_recv.at[i, 1], y_prev),
        ]
        plain = [
            copy_to(block(yp, half), r2.at[i, 0, 1], r_send.at[i, 2], r_recv.at[i, 2], y_next),
            copy_to(block(ym, 0), r2.at[i, 1, 0], r_send.at[i, 3], r_recv.at[i, 3], y_prev),
        ]
        for copy in one + plain:
            go(copy)
        return one, plain

    def ring_middle(i, block, half, one):
        out = []
        for d, (copy, near, device, lo) in enumerate(
            zip(one, (yp, ym), (y_next, y_prev), (0, half))
        ):
            copy.wait_recv()
            stage[i, d] = (block(near, lo)[...].astype(F32) + r1[i, d].astype(F32)).astype(BF)
            summed = copy_to(
                stage.at[i, d], r2.at[i, d, d], r_send.at[i, 4 + d], r_recv.at[i, 4 + d], device
            )
            go(summed)
            out.append(summed)
        return out

    def ring_end(i, copies, mine):
        for copy in copies:
            copy.wait_recv()
        return [
            mine(k) + r2[i, 0, k].astype(F32) + r2[i, 1, k].astype(F32) for k in range(2)
        ]

    def part_block(start, half):
        def block(y_at, lo):
            return part.at[:, y_at, :, pl.ds(start + lo, half)]
        return block

    def sum_block(half):
        def block(y_at, lo):
            return zf_sum.at[0, :, y_at, :, pl.ds(lo, half)]
        return block

    half = 512
    rings = []
    for i, (start, width) in enumerate(Y_FIRST):
        project(start, width)
        rings.append(ring_start(i, part_block(start, half), half))
    text_copies = text_sum(text_copies)
    second = []
    for i, (start, width) in enumerate(Y_FIRST):
        second.append(ring_middle(i, part_block(start, half), half, rings[i][0]))
    text_spread_mate()

    zf_copies[0].wait_recv()
    start = Z_FIRST[0][0]
    for k in range(4):
        zf_sum[0, 0, k] = (
            part[zl, k, :, start:start + 1024].astype(F32) + zf_in[0, k].astype(F32)
        ).astype(BF)

    def z_block(y_at, lo):
        return zf_sum.at[0, 0, y_at, :, pl.ds(lo, half)]

    i_z = len(Y_FIRST)
    one_z = [
        copy_to(z_block(yo, 0), r1.at[i_z, 0, 0], r_send.at[i_z, 0], r_recv.at[i_z, 0], y_next),
        copy_to(z_block(yo, half), r1.at[i_z, 1, 0], r_send.at[i_z, 1], r_recv.at[i_z, 1], y_prev),
    ]
    plain_z = [
        copy_to(z_block(yp, half), r2.at[i_z, 0, 1, 0], r_send.at[i_z, 2], r_recv.at[i_z, 2], y_next),
        copy_to(z_block(ym, 0), r2.at[i_z, 1, 0, 0], r_send.at[i_z, 3], r_recv.at[i_z, 3], y_prev),
    ]
    for copy in one_z + plain_z:
        go(copy)

    text_spread_inter()

    z_copies = []
    own_sums = []
    for i, (start, width) in enumerate(Y_FIRST):
        def mine(k, start=start):
            return part[:, y, :, start + k * half:start + (k + 1) * half].astype(F32)
        sums = ring_end(i, rings[i][1] + second[i], mine)
        for k in range(2):
            zs[i, :, :, k * half:(k + 1) * half] = sums[k].astype(BF)
            vout_ref[:, start + k * half:start + (k + 1) * half] = jnp.where(zl == 0, sums[k][0], sums[k][1])
        copy = copy_to(zs.at[i, 1 - zl], zr.at[i], zx_sem.at[0, i], zx_sem.at[1, i], z_pair)
        go(copy)
        z_copies.append(copy)

    second_z = []
    for d, (copy, near, device, lo) in enumerate(
        zip(one_z, (yp, ym), (y_next, y_prev), (0, half))
    ):
        copy.wait_recv()
        stage[i_z, d, 0] = (z_block(near, lo)[...].astype(F32) + r1[i_z, d, 0].astype(F32)).astype(BF)
        summed = copy_to(
            stage.at[i_z, d, 0], r2.at[i_z, d, d, 0], r_send.at[i_z, 4 + d], r_recv.at[i_z, 4 + d], device
        )
        go(summed)
        second_z.append(summed)
    text_spread_sib()
    for copy in plain_z + second_z:
        copy.wait_recv()
    for k in range(2):
        start = Z_FIRST[0][0] + k * half
        vout_ref[:, start:start + half] = (
            zf_sum[0, 0, y, :, k * half:(k + 1) * half].astype(F32)
            + r2[i_z, 0, k, 0].astype(F32)
            + r2[i_z, 1, k, 0].astype(F32)
        )
    for i, (start, width) in enumerate(Y_FIRST):
        z_copies[i].wait_recv()
        vout_ref[:, start:start + width] = vout_ref[:, start:start + width] + zr[i].astype(F32)
    text_finish()

    for copy in sends:
        copy.wait_send()

    @pl.when(v_send)
    def _():
        for t, j in pieces:
            to_vert(t, j).wait_send()

    @pl.when(v_recv)
    def _():
        for t, j in pieces:
            to_vmate(t, j).wait_send()
            to_sib(VERT, t, j).wait_send()
            to_sib(VMATE, t, j).wait_send()


def body(video_q, video_k, video_v, text_q, text_k, text_v, band_start, text_mask, video_proj, text_proj):
    dma = pltpu.SemaphoreType.DMA
    vmem = pltpu.VMEM
    any_spec = pl.BlockSpec(memory_space=pl.ANY)
    vmem_spec = pl.BlockSpec(memory_space=pltpu.VMEM)
    smem_spec = pl.BlockSpec(memory_space=pltpu.SMEM)
    n_y = len(Y_FIRST)
    return pl.pallas_call(
        kernel,
        name="joint_attention",
        out_shape=(
            jax.ShapeDtypeStruct((32, WIDTH), F32),
            jax.ShapeDtypeStruct((32, WIDTH), F32),
        ),
        in_specs=[any_spec] * 6 + [smem_spec, vmem_spec, any_spec, any_spec],
        out_specs=(vmem_spec, vmem_spec),
        scratch_shapes=[
            vmem((4, 2, 256, LANES), BF),
            vmem((4, 2, 256, LANES), BF),
            vmem((4, 2, 256, LANES), BF),
            vmem((256, LANES), BF),
            vmem((256, LANES), BF),
            vmem((256, LANES), BF),
            vmem((256, LANES), BF),
            vmem((LANES, WIDTH), BF),
            vmem((LANES, LANES), BF),
            vmem((HEADS_HERE, 256, 2 * HD), F32),
            vmem((HEADS_HERE, 256, HD), F32),
            vmem((256, LANES), BF),
            vmem((2, 4, 32, WIDTH), BF),
            dma((11, 2, CHUNKS)),
            dma((12, 2, CHUNKS)),
            dma((8,)),
            vmem((2, 8, 16, 512), BF),
            vmem((8, 16, 512), BF),
            vmem((2, 4, 16, 512), BF),
            vmem((4, 16, 512), BF),
            vmem((2, 2, 16, 512), BF),
            vmem((2, 16, 512), BF),
            vmem((4, 8, 512), F32),
            vmem((4, 8, 512), F32),
            vmem((8, 8, LANES), F32),
            vmem((8, 8, LANES), F32),
            vmem((7, 8, LANES), F32),
            vmem((2, 2, 4, 2, 8, LANES), F32),
            dma((6,)),
            dma((4,)),
            dma((4,)),
            dma((7,)),
            dma((7,)),
            dma((7,)),
            dma((7,)),
            dma((7,)),
            dma((7,)),
            vmem((1, 4, 32, 1024), BF),
            vmem((1, 1, 4, 32, 1024), BF),
            vmem((n_y + 1, 2, 2, 32, 512), BF),
            vmem((n_y + 1, 2, 2, 2, 32, 512), BF),
            vmem((n_y + 1, 2, 2, 32, 512), BF),
            vmem((n_y, 2, 32, 1024), BF),
            vmem((n_y, 32, 1024), BF),
            dma((2, 1)),
            dma((n_y + 1, 6)),
            dma((n_y + 1, 6)),
            dma((2, n_y)),
        ],
        compiler_params=pltpu.CompilerParams(
            collective_id=0, has_side_effects=True, vmem_limit_bytes=56 * 2**20
        ),
        cost_estimate=pl.CostEstimate(flops=2_000_000_000, bytes_accessed=8_000_000, transcendentals=2_500_000),
    )(
        video_q, video_k, video_v, text_q, text_k, text_v, band_start, text_mask.reshape(1, TXT),
        video_proj, text_proj,
    )


def solution(mesh):
    return jax.shard_map(
        body,
        mesh=mesh,
        in_specs=(
            P("frm", "head"), P("frm", "head"), P("frm", "head"),
            P(None, "head"), P(None, "head"), P(None, "head"),
            P("frm"), P(), P("head", None), P("head", None),
        ),
        out_specs=(P(("frm", "head"), None), P("head", None)),
        check_vma=False,
    )
```

```python
import math

import jax
import jax.numpy as jnp
from jax import lax
from jax.experimental import pallas as pl
from jax.experimental.pallas import tpu as pltpu
from jax.sharding import PartitionSpec as P

HD = 128
TXT = 256
BANDS = 4
HEADS_HERE = 3
LANES = HEADS_HERE * HD
WIDTH = 3072
MESH = pl.DeviceIdType.MESH
BF = jnp.bfloat16
F32 = jnp.float32
FACTOR = math.log2(math.e) / math.sqrt(HD)
DEAD = -1e30
CHUNKS = 4
OWN, MATE, OPP, INTER, VMATE, VERT = range(6)
FAR = ((1, 2), (1, 3))
OPP_BY_MATE = ((1, 0), (1, 1), (1, 2))
PART = 768
HALF = PART // 2


def dot_nt(a, b):
    return lax.dot_general(a, b, (((1,), (1,)), ((), ())), preferred_element_type=F32)


def dot_nn(a, b):
    return jnp.dot(a, b, preferred_element_type=F32)


def with_ones(values):
    return jnp.concatenate([values, jnp.ones(values.shape, BF)], axis=1)


def kernel(
    vq_hbm, vk_hbm, vv_hbm, tq_hbm, tk_hbm, tv_hbm, band_hbm, mask_hbm, vproj_hbm, tproj_hbm,
    vout_ref, tout_ref,
    band_ref, mask_ref, k_a, k_b, k_c, v_a, v_b, v_c, vq, tq, tk, tv, vproj, tproj, state_o, state_m, weights_ref, attn, wpair, relay,
    kv_send, kv_recv, sib_recv, relay_recv, load_sem,
    t_a, t_ar, t_b, t_br, t_c, t_cr, t_z, t_zr, t_rows, t_sums, t_sumr, t_out,
    ta_sem, tz_sem, tg_sem, ts_sem, to_sem,
    swap_in, keep, y_out, y_in, z_out, z_in,
    w_sem, swap_sem, y_send, y_recv, z_send, z_recv,
):
    frm = lax.axis_index("frm")
    head = lax.axis_index("head")
    zh, x, c = frm // 8, (frm // 2) % 4, frm % 2
    zl, y = head // 4, head % 4
    xr, xo = x // 2, x % 2

    def at(zh_, x_, c_):
        return {"frm": zh_ * 8 + x_ * 2 + c_, "head": head}

    def at_head(zl_, y_):
        return {"frm": frm, "head": zl_ * 4 + y_}

    x_mate = x + 1 - 2 * xo
    sib = at(zh, x, 1 - c)
    mate = at(zh, x_mate, c)
    inter = at(zh, 3 - x, c)
    z_pair = at_head(1 - zl, y)
    y_of = (y + 1 - 2 * (y % 2), 3 - y)
    y_opp = (y + 2) % 4
    y_pair = (at_head(zl, y_of[0]), at_head(zl, y_of[1]))
    zh_to = zh + 1 - 2 * xr
    v_send = (zh_to >= 0) & (zh_to <= 3)
    zh_from = zh - 1 + 2 * xr
    v_recv = (zh_from >= 0) & (zh_from <= 3)
    vert = at(jnp.clip(zh_to, 0, 3), x, c)
    far = at(jnp.clip(zh_from, 0, 3), x, c)

    def copy_to(src, dst, send, recv, device):
        return pltpu.make_async_remote_copy(
            src_ref=src, dst_ref=dst, send_sem=send, recv_sem=recv,
            device_id=device, device_id_type=MESH,
        )

    loads = []

    def load(src, dst):
        copy = pltpu.make_async_copy(src, dst, load_sem.at[len(loads)])
        copy.start()
        loads.append(copy)
        return copy

    load_own = [load(vk_hbm, k_a.at[0]), load(vv_hbm, v_a.at[0])]
    load_text = [
        load(tq_hbm, tq), load(tk_hbm, tk), load(tv_hbm, tv), load(mask_hbm, mask_ref), load(band_hbm, band_ref)
    ]
    load_q = load(vq_hbm, vq)
    load_vproj = load(vproj_hbm, vproj)
    load_tproj = load(tproj_hbm.at[:, pl.ds(pl.multiple_of(x * 768, 768), 768)], tproj)

    frm_partners = [sib]
    frm_partners += [at((zh + d) % 4, x, c) for d in range(1, 4)]
    frm_partners += [at(zh, (x + d) % 4, c) for d in range(1, 4)]
    head_partners = [
        ((zl + dz) % 2, (y + dy) % 4) for dz in range(2) for dy in range(4) if (dz, dy) != (0, 0)
    ]
    barrier = pltpu.get_barrier_semaphore()
    with jax.named_scope("barrier"):
        for device in frm_partners + [at_head(a, b) for a, b in head_partners]:
            pl.semaphore_signal(barrier, inc=1, device_id=device, device_id_type=MESH)
        pl.semaphore_wait(barrier, len(frm_partners) + len(head_partners))

    rows = 256 // CHUNKS
    sends = []

    def kv_copy(kind, t, j, src_slot, dst_slot, device, src=None):
        rng = pl.ds(j * rows, rows)
        return copy_to(
            kv_of[t][src_slot // 4].at[src_slot % 4, rng] if src is None else src.at[rng],
            kv_of[t][dst_slot // 4].at[dst_slot % 4, rng],
            kv_send.at[kind],
            sib_recv.at[dst_slot // 2, t] if dst_slot % 2 else kv_recv.at[dst_slot // 2, t, j],
            device,
        )

    kv_of = ((k_a, k_b, k_c), (v_a, v_b, v_c))
    pieces = [(t, j) for t in range(2) for j in range(CHUNKS)]
    own_hbm = (vk_hbm, vv_hbm)

    def to_mate(t, j):
        return kv_copy(0, t, j, 0, 2 * MATE, mate, own_hbm[t])

    def to_inter(t, j):
        return kv_copy(1, t, j, 0, 2 * INTER, inter, own_hbm[t])

    def to_opp(t, j):
        if (t, j) in OPP_BY_MATE:
            return kv_copy(2, t, j, 2 * INTER, 2 * OPP, mate)
        return kv_copy(2, t, j, 2 * MATE, 2 * OPP, inter)

    def to_far(which, t, j):
        k = FAR.index((t, j))
        rng = pl.ds(j * rows, rows)
        return copy_to(
            own_hbm[t].at[rng] if which == 0 else kv_of[t][0].at[2 * MATE, rng],
            relay.at[which, k], kv_send.at[11 + which], relay_recv.at[which, k], far,
        )

    def to_relayed(which, t, j):
        k = FAR.index((t, j))
        role = (VERT, VMATE)[which]
        return copy_to(
            relay.at[which, k], kv_of[t][2].at[2 * role % 4, pl.ds(j * rows, rows)],
            kv_send.at[13 + which], kv_recv.at[role, t, j], inter,
        )

    def to_vert(t, j):
        return kv_copy(3, t, j, 2 * INTER, 2 * VERT, vert)

    def to_vmate(t, j):
        return kv_copy(4, t, j, 2 * VERT, 2 * VMATE, mate)

    def to_sib(role, t, j):
        return kv_copy(5 + role, t, j, 2 * role, 2 * role + 1, sib, own_hbm[t] if role == OWN else None)

    def go(copy):
        copy.start()
        sends.append(copy)

    def wait_bytes(ref, sem):
        copy_to(ref, ref, sem, kv_recv.at[0, 0, 0], sib).wait_send()

    def send_own(todo):
        for t, j in todo:
            to_inter(t, j).start()
            to_mate(t, j).start()
            to_sib(OWN, t, j).start()

    send_own(pieces[:CHUNKS])

    @pl.when(v_recv)
    def _():
        for t, j in FAR:
            to_far(0, t, j).start()

    def to_pair(pair):
        cols = pl.ds(pl.multiple_of(2 * PART * pair + PART * c, PART), PART)
        return copy_to(vproj_hbm.at[:, cols], wpair.at[pair, c], w_sem.at[0], w_sem.at[1 + pair], y_pair[pair])

    def pair_to_sib(pair):
        return copy_to(wpair.at[pair, c], wpair.at[pair, c], w_sem.at[3], w_sem.at[4], sib)

    for pair in range(2):
        to_pair(pair).start()

    for copy in load_own + load_text:
        copy.wait()
    lane = lax.broadcasted_iota(jnp.int32, (1, TXT), 1)
    text_bias = jnp.where(mask_ref[...] == 1, 0.0, DEAD)
    first_bias = jnp.where(frm == 0, text_bias, DEAD)

    def pack_stats(tops, totals):
        count = tops[0].shape[0]
        at_lane = lax.broadcasted_iota(jnp.int32, (count, HD), 1)
        packed = jnp.zeros((count, HD), F32)
        for h in range(HEADS_HERE):
            high = totals[h].astype(BF).astype(F32)
            packed = jnp.where(at_lane == h, tops[h], packed)
            packed = jnp.where(at_lane == 3 + h, high, packed)
            packed = jnp.where(at_lane == 6 + h, totals[h] - high, packed)
        return packed

    def text_partial():
        tops, totals, mixed = [], [], []
        for h in range(HEADS_HERE):
            cols = slice(h * HD, (h + 1) * HD)
            s_own = dot_nt(tq[:, cols], k_a[0, :, cols])
            s_text = dot_nt(tq[:, cols], tk[:, cols]) + first_bias
            top = jnp.maximum(
                jnp.max(s_own, axis=1, keepdims=True), jnp.max(s_text, axis=1, keepdims=True)
            ).astype(BF).astype(F32)
            base = top * FACTOR
            w_own = jnp.exp2(s_own * FACTOR - base).astype(BF)
            w_text = jnp.exp2(s_text * FACTOR - base).astype(BF)
            both = dot_nn(w_own, with_ones(v_a[0, :, cols])) + dot_nn(w_text, with_ones(tv[:, cols]))
            tops.append(top)
            totals.append(both[:, HD:HD + 1])
            mixed.append(both[:, :HD].astype(BF))
        stats = pack_stats(tops, totals).astype(BF)
        for h_to in range(8):
            for half in range(2):
                rng = slice(32 * h_to + 16 * half, 32 * h_to + 16 * half + 16)
                for h in range(HEADS_HERE):
                    t_a[half, h_to, :, h * HD:(h + 1) * HD] = mixed[h][rng]
                t_a[half, h_to, :, LANES:] = stats[rng]

    with jax.named_scope("text_partial"):
        text_partial()
    text_a = copy_to(t_a.at[1 - c], t_ar, ta_sem.at[0], ta_sem.at[1], sib)
    go(text_a)

    def merge(parts):
        parts = [p.astype(F32) for p in parts]
        out_tops, out_totals, out_mixed = [], [], []
        for h in range(HEADS_HERE):
            tops_h = [p[:, LANES + h:LANES + h + 1] for p in parts]
            top = tops_h[0]
            for other in tops_h[1:]:
                top = jnp.maximum(top, other)
            total, mix = 0.0, 0.0
            for p, top_p in zip(parts, tops_h):
                weight = jnp.exp2((top_p - top) * FACTOR)
                total_p = p[:, LANES + 3 + h:LANES + 4 + h] + p[:, LANES + 6 + h:LANES + 7 + h]
                total = total + total_p * weight
                mix = mix + p[:, h * HD:(h + 1) * HD] * weight
            out_tops.append(top)
            out_totals.append(total)
            out_mixed.append(mix)
        return out_tops, out_totals, out_mixed

    def merged(parts):
        out_tops, out_totals, out_mixed = merge(parts)
        return jnp.concatenate(out_mixed + [pack_stats(out_tops, out_totals)], axis=1)

    def slots_of_window():
        mid = c != xo
        pick_same = mid & (band_ref[0] == xo)
        return (0, jnp.where(mid, 3, 1), jnp.where(pick_same, 1, 2))

    def group_scores(g, with_text):
        slots = slots_of_window()
        for h in range(HEADS_HERE):
            cols = slice(h * HD, (h + 1) * HD)
            query = vq[:, cols]
            scores = [dot_nt(query, kv_of[0][g][s, :, cols]) for s in slots]
            if with_text:
                scores.append(dot_nt(query, tk[:, cols]) + text_bias)
            top = scores[0]
            for score in scores[1:]:
                top = jnp.maximum(top, score)
            top = jnp.max(top, axis=1, keepdims=True)
            base = top * FACTOR
            for i, score in enumerate(scores):
                weights_ref[g, h, i] = jnp.exp2(score * FACTOR - base).astype(BF)
            state_m[g, h] = jnp.broadcast_to(top, (256, HD))

    def group_values(g, with_text):
        slots = slots_of_window()
        for h in range(HEADS_HERE):
            cols = slice(h * HD, (h + 1) * HD)
            total = dot_nn(weights_ref[g, h, 0], with_ones(kv_of[1][g][slots[0], :, cols]))
            for i in (1, 2):
                total = total + dot_nn(weights_ref[g, h, i], with_ones(kv_of[1][g][slots[i], :, cols]))
            if with_text:
                total = total + dot_nn(weights_ref[g, h, 3], with_ones(tv[:, cols]))
            state_o[g, h] = total

    def join_groups():
        for h in range(HEADS_HERE):
            tops = [state_m[g, h] for g in range(3)]
            top = jnp.maximum(jnp.maximum(tops[0], tops[1]), tops[2])
            mix, total = 0.0, 0.0
            for g in range(3):
                factor = jnp.exp2((tops[g] - top) * FACTOR)
                mix = mix + state_o[g, h, :, :HD] * factor
                total = total + state_o[g, h, :, HD:] * factor
            attn[:, :, :, h * HD:(h + 1) * HD] = (mix / total).astype(BF).reshape(2, 4, 32, HD)

    def serve_inter(t, j):
        to_inter(t, j).wait_recv()
        to_sib(INTER, t, j).start()
        if (t, j) in OPP_BY_MATE:
            to_opp(t, j).start()

    def serve_mate(t, j):
        to_mate(t, j).wait_recv()
        if (t, j) in FAR:
            @pl.when(v_recv)
            def _():
                to_far(1, t, j).start()

        to_sib(MATE, t, j).start()
        if (t, j) not in OPP_BY_MATE:
            to_opp(t, j).start()

    def pass_own(t, j):
        @pl.when(v_send)
        def _():
            to_far(0, t, j).wait_recv()
            to_relayed(0, t, j).start()

    def pass_mate(t, j):
        @pl.when(v_send)
        def _():
            to_far(1, t, j).wait_recv()
            to_relayed(1, t, j).start()

    def serve_far(t, j):
        @pl.when(v_recv)
        def _():
            to_relayed(0, t, j).wait_recv()
            to_sib(VERT, t, j).start()
            to_relayed(1, t, j).wait_recv()
            to_sib(VMATE, t, j).start()

    def send_vert(t, j):
        @pl.when(v_send)
        def _():
            to_vert(t, j).start()

    def text_step_a():
        text_a.wait_recv()
        for h_to in range(8):
            t_b[h_to // 4, h_to % 4] = merged([t_a[c, h_to], t_ar[h_to]]).astype(BF)
        copy = copy_to(t_b.at[1 - xr], t_br, ta_sem.at[2], ta_sem.at[3], inter)
        go(copy)
        return copy

    def text_step_b(copy):
        copy.wait_recv()
        for k in range(4):
            t_c[k // 2, k % 2] = merged([t_b[xr, k], t_br[k]]).astype(BF)
        copy = copy_to(t_c.at[1 - xo], t_cr, ta_sem.at[4], ta_sem.at[5], mate)
        go(copy)
        return copy

    def text_step_c(copy):
        copy.wait_recv()
        for k in range(2):
            t_z[k] = merged([t_c[xo, k], t_cr[k]]).astype(BF)
        for dz in range(1, 4):
            copy_to(t_z, t_zr.at[dz], tz_sem.at[0], tz_sem.at[1], at((zh + dz) % 4, x, c)).start()

    def text_step_z():
        block = t_zr.at[pl.ds(1, 3)]
        copy_to(block, block, tz_sem.at[0], tz_sem.at[1], sib).wait_recv()
        for k in range(2):
            _, sums, mix = merge([t_z[k], t_zr[1, k], t_zr[2, k], t_zr[3, k]])
            for h in range(HEADS_HERE):
                t_rows[x, k, :, h * HD:(h + 1) * HD] = (mix[h] / sums[h]).astype(BF)
        for dx in range(1, 4):
            copy_to(t_rows.at[x], t_rows.at[x], tg_sem.at[0], tg_sem.at[1], at(zh, (x + dx) % 4, c)).start()

    def text_gather():
        block = t_rows.at[pl.ds(0, 3)]
        copy_to(block, block, tg_sem.at[0], tg_sem.at[1], sib).wait_recv()
        load_tproj.wait()
        rows_all = t_rows[...].reshape(128, LANES)
        product = dot_nn(rows_all, tproj[...]).astype(BF)
        for k in range(8):
            t_sums[k] = product[16 * k:16 * k + 16]
        for k, (a, b) in enumerate(head_partners):
            copy_to(t_sums.at[a * 4 + b], t_sumr.at[k], ts_sem.at[0], ts_sem.at[1], at_head(a, b)).start()

    def text_sum():
        copy_to(t_sumr, t_sumr, ts_sem.at[0], ts_sem.at[1], sib).wait_recv()
        total = t_sums[head].astype(F32)
        for k in range(7):
            total = total + t_sumr[k].astype(F32)
        t_out[c, x] = total
        for dx in range(1, 4):
            block = t_out.at[c, x]
            copy_to(block, block, to_sem.at[0], to_sem.at[1], at(zh, (x + dx) % 4, c)).start()

    def text_spread_sib():
        block = t_out.at[c, pl.ds(0, 3)]
        copy_to(block, block, to_sem.at[0], to_sem.at[1], sib).wait_recv()
        go(copy_to(t_out.at[c], t_out.at[c], to_sem.at[2], to_sem.at[3], sib))

    def text_finish():
        block = t_out.at[1 - c]
        copy_to(block, block, to_sem.at[2], to_sem.at[3], sib).wait_recv()
        for cc in range(2):
            for k in range(4):
                tout_ref[16 * cc:16 * cc + 16, k * 768:(k + 1) * 768] = t_out[cc, k]

    def serve_vert(t, j):
        @pl.when(v_recv)
        def _():
            to_vert(t, j).wait_recv()
            to_vmate(t, j).start()
            to_sib(VERT, t, j).start()

    def serve_vmate(t, j):
        @pl.when(v_recv)
        def _():
            to_vmate(t, j).wait_recv()
            to_sib(VMATE, t, j).start()

    def wait_sib(roles, t):
        for role in roles:
            block = kv_of[t][(2 * role + 1) // 4].at[(2 * role + 1) % 4]
            copy_to(block, block, kv_send.at[0], sib_recv.at[role, t], sib).wait_recv()

    def wait_sib_vert(t):
        @pl.when(v_recv)
        def _():
            wait_sib((VERT, VMATE), t)

    def serve_opp(t, j):
        to_opp(t, j).wait_recv()
        to_sib(OPP, t, j).start()

    scope = jax.named_scope
    def many(step, todo):
        with scope(step.__name__):
            for p in todo:
                step(*p)

    def part_of(todo, lo, hi):
        return todo[lo * CHUNKS // 4:hi * CHUNKS // 4]

    def first_hop(p, near):
        many(serve_inter, [p])
        if near:
            many(send_vert, [p])
        many(serve_mate, [p])

    k0, k1, k2, k3, v0, v1, v2, v3 = pieces
    first_hop(k0, True)
    with scope("text_sibling_merge"):
        text_copy = text_step_a()
        send_own(pieces[CHUNKS:])
    for p in (k1, k2, k3):
        first_hop(p, True)
    with scope("text_inter_merge"):
        text_copy = text_step_b(text_copy)
    first_hop(v0, True)
    first_hop(v1, True)
    many(pass_own, FAR)
    first_hop(v2, False)
    first_hop(v3, False)
    many(serve_vert, [k0, k1])
    with scope("text_mate_merge"):
        text_step_c(text_copy)
    with scope("wait_own_frame"):
        load_q.wait()
        wait_sib((OWN, MATE), 0)
        wait_sib((OWN, MATE), 1)
    with scope("own_frame"):
        group_scores(0, True)
        group_values(0, True)
    many(serve_vert, [k2, k3])
    many(serve_vmate, [k0])
    many(serve_opp, [k0, k1])
    many(pass_mate, FAR)
    with scope("projection_halves"):
        for pair in range(2):
            to_pair(pair).wait_recv()
            pair_to_sib(pair).start()
    many(serve_vert, [v0])
    many(serve_opp, [k2, k3])
    many(serve_vmate, [k1, k2])
    with scope("wait_beside_keys"):
        wait_sib((OPP, INTER), 0)
    with scope("frame_beside_scores"):
        group_scores(1, False)
    many(serve_vmate, [k3])
    many(serve_vert, [v1])
    with scope("wait_across_keys"):
        wait_sib_vert(0)
    with scope("frame_across_scores"):
        @pl.when(v_recv)
        def _():
            group_scores(2, False)

        @pl.when(jnp.logical_not(v_recv))
        def _():
            state_m[2] = jnp.full((HEADS_HERE, 256, HD), DEAD, F32)
            state_o[2] = jnp.zeros((HEADS_HERE, 256, 2 * HD), F32)
    many(serve_opp, [v0, v1, v2, v3])
    many(serve_vmate, [v0])
    with scope("text_z_merge"):
        text_step_z()
    many(serve_far, FAR)
    many(serve_vmate, [v1])
    with scope("wait_beside_values"):
        wait_sib((OPP, INTER), 1)
    with scope("frame_beside_values"):
        group_values(1, False)
    with scope("wait_across_values"):
        wait_sib_vert(1)
    with scope("frame_across_values"):
        @pl.when(v_recv)
        def _():
            group_values(2, False)
    with scope("join_groups"):
        join_groups()
    swap_own, swap_pair = [attn.at[:, y_of[0]], attn.at[:, y_of[1]]], attn.at[:, y_opp]
    for pair in range(2):
        copy_to(swap_own[pair], swap_in.at[pair, 0], swap_sem.at[0], swap_sem.at[1 + pair], y_pair[pair]).start()
        copy_to(swap_pair, swap_in.at[pair, 1], swap_sem.at[0], swap_sem.at[1 + pair], y_pair[pair]).start()

    with scope("text_gather"):
        text_gather()

    def own_rows(pair):
        return jnp.concatenate(
            [attn[:, y].reshape(64, LANES), attn[:, y_of[1 - pair]].reshape(64, LANES)], axis=0
        )

    with scope("project_own"):
        load_vproj.wait()
        for pair in range(2):
            rows_here = own_rows(pair)
            for q in range(2):
                lo = (2 * pair + q) * PART
                product = dot_nn(rows_here, vproj[:, lo:lo + PART])
                keep[pair, 2 * q], keep[pair, 2 * q + 1] = product[:, :HALF], product[:, HALF:]
        copy_to(wpair.at[0], wpair.at[0], w_sem.at[3], w_sem.at[4], sib).wait_recv()
    parts_of = [(pair, q) for q in range(4) for pair in range(2)]
    for pair in range(2):
        with scope("swap_wait"):
            copy_to(swap_in.at[pair], swap_in.at[pair], swap_sem.at[0], swap_sem.at[1 + pair], sib).wait_recv()
    for pair, q in parts_of:
        if q % 2 == 0:
            with scope("project_pair"):
                product = dot_nn(swap_in[pair].reshape(128, LANES), wpair[pair, q // 2])
                for k in range(2):
                    total = keep[pair, q + k] + product[:, k * HALF:(k + 1) * HALF]
                    y_out[pair, q + k] = total[64:].astype(BF)
                    keep[pair, q + k, :64] = total[:64]
                    copy_to(
                        y_out.at[pair, q + k], y_in.at[pair, q + k], y_send.at[0], y_recv.at[pair, q + k],
                        y_pair[1 - pair],
                    ).start()
    for pair, q in parts_of:
        if (pair, q) == parts_of[4]:
            with scope("text_sum"):
                text_sum()
        with scope("y_wait"):
            came = y_in.at[pair, q]
            copy_to(came, came, y_send.at[0], y_recv.at[pair, q], sib).wait_recv()
        with scope("y_sum"):
            lo = (4 * pair + q) * HALF
            total = keep[pair, q, :64] + y_in[pair, q].astype(F32)
            vout_ref[:, lo:lo + HALF] = jnp.where(zl == 0, total[:32], total[32:])
            z_out[pair, q] = jnp.where(zl == 0, total[32:], total[:32]).astype(BF)
        copy_to(z_out.at[pair, q], z_in.at[pair, q], z_send.at[0], z_recv.at[pair, q], z_pair).start()
    for pair, q in parts_of:
        if (pair, q) == parts_of[4]:
            with scope("text_spread_sib"):
                text_spread_sib()
        with scope("z_wait"):
            came = z_in.at[pair, q]
            copy_to(came, came, z_send.at[0], z_recv.at[pair, q], sib).wait_recv()
        lo = (4 * pair + q) * HALF
        vout_ref[:, lo:lo + HALF] = vout_ref[:, lo:lo + HALF] + z_in[pair, q].astype(F32)
    with scope("text_finish"):
        text_finish()

    with scope("wait_sends"):
        for copy in sends:
            copy.wait_send()

        whole = k_a.at[pl.ds(0, 2)]
        for kind in (0, 1, 2, 5 + OWN, 5 + MATE, 5 + OPP, 5 + INTER):
            wait_bytes(whole, kv_send.at[kind])

        most, quarter = k_a.at[pl.ds(0, 3), pl.ds(0, 128)], k_a.at[0, pl.ds(0, 128)]

        @pl.when(v_send)
        def _():
            wait_bytes(most, kv_send.at[3])
            wait_bytes(quarter, kv_send.at[13])
            wait_bytes(quarter, kv_send.at[14])

        @pl.when(v_recv)
        def _():
            wait_bytes(most, kv_send.at[4])
            wait_bytes(whole, kv_send.at[5 + VERT])
            wait_bytes(whole, kv_send.at[5 + VMATE])
            wait_bytes(quarter, kv_send.at[11])
            wait_bytes(quarter, kv_send.at[12])

        wait_bytes(t_zr.at[pl.ds(1, 3)], tz_sem.at[0])
        wait_bytes(t_rows.at[pl.ds(0, 3)], tg_sem.at[0])
        wait_bytes(t_sumr, ts_sem.at[0])
        wait_bytes(t_out.at[0, pl.ds(0, 3)], to_sem.at[0])
        wait_bytes(wpair.at[0], w_sem.at[0])
        wait_bytes(wpair.at[0], w_sem.at[3])
        wait_bytes(swap_in, swap_sem.at[0])
        wait_bytes(y_in, y_send.at[0])
        wait_bytes(z_in, z_send.at[0])


def store(video, text, video_out, text_out, sems):
    copies = [
        pltpu.make_async_copy(video, video_out, sems.at[0]),
        pltpu.make_async_copy(text, text_out, sems.at[1]),
    ]
    for copy in copies:
        copy.start()
    for copy in copies:
        copy.wait()


def body(video_q, video_k, video_v, text_q, text_k, text_v, band_start, text_mask, video_proj, text_proj):
    dma = pltpu.SemaphoreType.DMA
    vmem = pltpu.VMEM
    hbm_spec = pl.BlockSpec(memory_space=pltpu.HBM)
    vmem_spec = pl.BlockSpec(memory_space=pltpu.VMEM)
    outs = pl.pallas_call(
        kernel,
        name="joint_attention",
        out_shape=(pltpu.VMEM((32, WIDTH), F32), pltpu.VMEM((32, WIDTH), F32)),
        in_specs=[hbm_spec] * 10,
        out_specs=(vmem_spec, vmem_spec),
        scratch_shapes=[
            pltpu.SMEM((1,), jnp.int32),
            vmem((1, TXT), jnp.int32),
            *[vmem((4, 256, LANES), BF) for _ in range(6)],
            vmem((256, LANES), BF),
            vmem((256, LANES), BF),
            vmem((256, LANES), BF),
            vmem((256, LANES), BF),
            vmem((LANES, WIDTH), BF),
            vmem((LANES, 768), BF),
            vmem((3, HEADS_HERE, 256, 2 * HD), F32),
            vmem((3, HEADS_HERE, 256, HD), F32),
            vmem((3, HEADS_HERE, 4, 256, 256), BF),
            vmem((2, 4, 32, LANES), BF),
            vmem((2, 2, LANES, PART), BF),
            vmem((2, len(FAR), 256 // CHUNKS, LANES), BF),
            dma((15,)),
            dma((6, 2, CHUNKS)),
            dma((6, 2)),
            dma((2, len(FAR))),
            dma((10,)),
            vmem((2, 8, 16, 512), BF),
            vmem((8, 16, 512), BF),
            vmem((2, 4, 16, 512), BF),
            vmem((4, 16, 512), BF),
            vmem((2, 2, 16, 512), BF),
            vmem((2, 16, 512), BF),
            vmem((2, 16, 512), BF),
            vmem((4, 2, 16, 512), BF),
            vmem((4, 2, 16, LANES), BF),
            vmem((8, 16, 768), BF),
            vmem((7, 16, 768), BF),
            vmem((2, 4, 16, 768), F32),
            dma((6,)),
            dma((2,)),
            dma((2,)),
            dma((2,)),
            dma((4,)),
            vmem((2, 2, 2, 32, LANES), BF),
            vmem((2, 4, 128, HALF), F32),
            vmem((2, 4, 64, HALF), BF),
            vmem((2, 4, 64, HALF), BF),
            vmem((2, 4, 32, HALF), BF),
            vmem((2, 4, 32, HALF), BF),
            dma((5,)),
            dma((3,)),
            dma((1,)),
            dma((2, 4)),
            dma((1,)),
            dma((2, 4)),
        ],
        compiler_params=pltpu.CompilerParams(
            collective_id=0, has_side_effects=True, vmem_limit_bytes=56 * 2**20
        ),
        cost_estimate=pl.CostEstimate(flops=2_000_000_000, bytes_accessed=8_000_000, transcendentals=2_500_000),
    )(
        video_q, video_k, video_v, text_q, text_k, text_v, band_start, text_mask.reshape(1, TXT),
        video_proj, text_proj,
    )
    result = jax.ShapeDtypeStruct((32, WIDTH), F32)
    return pl.pallas_call(
        store,
        name="store",
        out_shape=(result, result),
        in_specs=[vmem_spec, vmem_spec],
        out_specs=(hbm_spec, hbm_spec),
        scratch_shapes=[dma((2,))],
    )(*[pltpu.with_memory_space_constraint(out, pltpu.VMEM) for out in outs])


def solution(mesh):
    return jax.shard_map(
        body,
        mesh=mesh,
        in_specs=(
            P("frm", "head"), P("frm", "head"), P("frm", "head"),
            P(None, "head"), P(None, "head"), P(None, "head"),
            P("frm"), P(), P("head", None), P("head", None),
        ),
        out_specs=(P(("frm", "head"), None), P("head", None)),
        check_vma=False,
    )
```

```python
import math

import jax
import jax.numpy as jnp
from jax import lax
from jax.experimental import pallas as pl
from jax.experimental.pallas import tpu as pltpu
from jax.sharding import PartitionSpec as P

HD = 128
TXT = 256
BANDS = 4
HEADS_HERE = 3
LANES = HEADS_HERE * HD
WIDTH = 3072
MESH = pl.DeviceIdType.MESH
BF = jnp.bfloat16
F32 = jnp.float32
FACTOR = math.log2(math.e) / math.sqrt(HD)
DEAD = -1e30
CHUNKS = 4
OWN, MATE, OPP, INTER, VMATE, VERT = range(6)
PER = CHUNKS // 4


def quarter(t, k):
    return tuple((t, k * PER + i) for i in range(PER))


FAR = quarter(1, 2) + quarter(1, 3)
OPP_BY_MATE = quarter(1, 0) + quarter(1, 1) + quarter(1, 2)
PART = 768
HALF = PART // 2


def dot_nt(a, b):
    return lax.dot_general(a, b, (((1,), (1,)), ((), ())), preferred_element_type=F32)


def dot_nn(a, b):
    return jnp.dot(a, b, preferred_element_type=F32)


def with_ones(values):
    return jnp.concatenate([values, jnp.ones(values.shape, BF)], axis=1)


def kernel(
    vq_hbm, vk_hbm, vv_hbm, tq_hbm, tk_hbm, tv_hbm, band_hbm, mask_hbm, vproj_hbm, tproj_hbm,
    vout_ref, tout_ref,
    band_ref, mask_ref, k_a, k_b, k_c, v_a, v_b, v_c, vq, tq, tk, tv, vproj, tproj, state_o, state_m, weights_ref, attn, wpair, relay,
    kv_send, kv_recv, sib_recv, relay_recv, load_sem,
    t_a, t_ar, t_b, t_br, t_c, t_cr, t_z, t_zr, t_rows, t_sums, t_sumr, t_out,
    ta_sem, tz_sem, tg_sem, ts_sem, to_sem,
    swap_in, keep, y_out, y_in, z_out, z_in,
    w_sem, swap_sem, y_send, y_recv, z_send, z_recv,
):
    frm = lax.axis_index("frm")
    head = lax.axis_index("head")
    zh, x, c = frm // 8, (frm // 2) % 4, frm % 2
    zl, y = head // 4, head % 4
    xr, xo = x // 2, x % 2

    def at(zh_, x_, c_):
        return {"frm": zh_ * 8 + x_ * 2 + c_, "head": head}

    def at_head(zl_, y_):
        return {"frm": frm, "head": zl_ * 4 + y_}

    x_mate = x + 1 - 2 * xo
    sib = at(zh, x, 1 - c)
    mate = at(zh, x_mate, c)
    inter = at(zh, 3 - x, c)
    z_pair = at_head(1 - zl, y)
    y_of = (y + 1 - 2 * (y % 2), 3 - y)
    y_opp = (y + 2) % 4
    y_pair = (at_head(zl, y_of[0]), at_head(zl, y_of[1]))
    zh_to = zh + 1 - 2 * xr
    v_send = (zh_to >= 0) & (zh_to <= 3)
    zh_from = zh - 1 + 2 * xr
    v_recv = (zh_from >= 0) & (zh_from <= 3)
    vert = at(jnp.clip(zh_to, 0, 3), x, c)
    far = at(jnp.clip(zh_from, 0, 3), x, c)

    def copy_to(src, dst, send, recv, device):
        return pltpu.make_async_remote_copy(
            src_ref=src, dst_ref=dst, send_sem=send, recv_sem=recv,
            device_id=device, device_id_type=MESH,
        )

    loads = []

    def load(src, dst):
        copy = pltpu.make_async_copy(src, dst, load_sem.at[len(loads)])
        copy.start()
        loads.append(copy)
        return copy

    load_own = [load(vk_hbm, k_a.at[0]), load(vv_hbm, v_a.at[0])]
    load_text = [
        load(tq_hbm, tq), load(tk_hbm, tk), load(tv_hbm, tv), load(mask_hbm, mask_ref), load(band_hbm, band_ref)
    ]
    load_q = load(vq_hbm, vq)
    load_vproj = load(vproj_hbm, vproj)
    load_tproj = load(tproj_hbm.at[:, pl.ds(pl.multiple_of(x * 768, 768), 768)], tproj)

    frm_partners = [sib]
    frm_partners += [at((zh + d) % 4, x, c) for d in range(1, 4)]
    frm_partners += [at(zh, (x + d) % 4, c) for d in range(1, 4)]
    head_partners = [
        ((zl + dz) % 2, (y + dy) % 4) for dz in range(2) for dy in range(4) if (dz, dy) != (0, 0)
    ]
    barrier = pltpu.get_barrier_semaphore()
    with jax.named_scope("barrier"):
        for device in frm_partners + [at_head(a, b) for a, b in head_partners]:
            pl.semaphore_signal(barrier, inc=1, device_id=device, device_id_type=MESH)
        pl.semaphore_wait(barrier, len(frm_partners) + len(head_partners))

    rows = 256 // CHUNKS
    sends = []

    def kv_copy(kind, t, j, src_slot, dst_slot, device, src=None):
        rng = pl.ds(j * rows, rows)
        return copy_to(
            kv_of[t][src_slot // 4].at[src_slot % 4, rng] if src is None else src.at[rng],
            kv_of[t][dst_slot // 4].at[dst_slot % 4, rng],
            kv_send.at[kind],
            sib_recv.at[dst_slot // 2, t] if dst_slot % 2 else kv_recv.at[dst_slot // 2, t, j],
            device,
        )

    kv_of = ((k_a, k_b, k_c), (v_a, v_b, v_c))
    pieces = [(t, j) for t in range(2) for j in range(CHUNKS)]
    own_hbm = (vk_hbm, vv_hbm)

    def to_mate(t, j):
        return kv_copy(0, t, j, 0, 2 * MATE, mate, own_hbm[t])

    def to_inter(t, j):
        return kv_copy(1, t, j, 0, 2 * INTER, inter, own_hbm[t])

    def to_opp(t, j):
        if (t, j) in OPP_BY_MATE:
            return kv_copy(2, t, j, 2 * INTER, 2 * OPP, mate)
        return kv_copy(2, t, j, 2 * MATE, 2 * OPP, inter)

    def to_far(which, t, j):
        k = FAR.index((t, j))
        rng = pl.ds(j * rows, rows)
        return copy_to(
            own_hbm[t].at[rng] if which == 0 else kv_of[t][0].at[2 * MATE, rng],
            relay.at[which, k], kv_send.at[11 + which], relay_recv.at[which, k], far,
        )

    def to_relayed(which, t, j):
        k = FAR.index((t, j))
        role = (VERT, VMATE)[which]
        return copy_to(
            relay.at[which, k], kv_of[t][2].at[2 * role % 4, pl.ds(j * rows, rows)],
            kv_send.at[13 + which], kv_recv.at[role, t, j], inter,
        )

    def to_vert(t, j):
        return kv_copy(3, t, j, 2 * INTER, 2 * VERT, vert)

    def to_vmate(t, j):
        return kv_copy(4, t, j, 2 * VERT, 2 * VMATE, mate)

    def to_sib(role, t, j):
        return kv_copy(5 + role, t, j, 2 * role, 2 * role + 1, sib, own_hbm[t] if role == OWN else None)

    def go(copy):
        copy.start()
        sends.append(copy)

    def wait_bytes(ref, sem):
        copy_to(ref, ref, sem, kv_recv.at[0, 0, 0], sib).wait_send()

    def send_own(todo_inter, todo_mate):
        for p_inter, p_mate in zip(todo_inter, todo_mate):
            to_inter(*p_inter).start()
            to_mate(*p_mate).start()
            to_sib(OWN, *p_mate).start()

    (k0, k1, k2, k3), (v0, v1, v2, v3) = [[quarter(t, k) for k in range(4)] for t in range(2)]
    order_inter = k0 + k1 + k2 + k3 + v0 + v1 + v2 + v3
    order_mate = k0 + k1 + v2 + v3 + k2 + k3 + v0 + v1
    send_own(order_inter[:CHUNKS], order_mate[:CHUNKS])

    @pl.when(v_recv)
    def _():
        for t, j in FAR:
            to_far(0, t, j).start()

    def to_pair(pair):
        cols = pl.ds(pl.multiple_of(2 * PART * pair + PART * c, PART), PART)
        return copy_to(vproj_hbm.at[:, cols], wpair.at[pair, c], w_sem.at[0], w_sem.at[1 + pair], y_pair[pair])

    def pair_to_sib(pair):
        return copy_to(wpair.at[pair, c], wpair.at[pair, c], w_sem.at[3], w_sem.at[4], sib)

    for pair in range(2):
        to_pair(pair).start()

    for copy in load_own + load_text:
        copy.wait()
    lane = lax.broadcasted_iota(jnp.int32, (1, TXT), 1)
    text_bias = jnp.where(mask_ref[...] == 1, 0.0, DEAD)
    first_bias = jnp.where(frm == 0, text_bias, DEAD)

    def pack_stats(tops, totals):
        count = tops[0].shape[0]
        at_lane = lax.broadcasted_iota(jnp.int32, (count, HD), 1)
        packed = jnp.zeros((count, HD), F32)
        for h in range(HEADS_HERE):
            high = totals[h].astype(BF).astype(F32)
            packed = jnp.where(at_lane == h, tops[h], packed)
            packed = jnp.where(at_lane == 3 + h, high, packed)
            packed = jnp.where(at_lane == 6 + h, totals[h] - high, packed)
        return packed

    def text_partial():
        tops, totals, mixed = [], [], []
        for h in range(HEADS_HERE):
            cols = slice(h * HD, (h + 1) * HD)
            s_own = dot_nt(tq[:, cols], k_a[0, :, cols])
            s_text = dot_nt(tq[:, cols], tk[:, cols]) + first_bias
            top = jnp.maximum(
                jnp.max(s_own, axis=1, keepdims=True), jnp.max(s_text, axis=1, keepdims=True)
            ).astype(BF).astype(F32)
            base = top * FACTOR
            w_own = jnp.exp2(s_own * FACTOR - base).astype(BF)
            w_text = jnp.exp2(s_text * FACTOR - base).astype(BF)
            both = dot_nn(w_own, with_ones(v_a[0, :, cols])) + dot_nn(w_text, with_ones(tv[:, cols]))
            tops.append(top)
            totals.append(both[:, HD:HD + 1])
            mixed.append(both[:, :HD].astype(BF))
        stats = pack_stats(tops, totals).astype(BF)
        for h_to in range(8):
            for half in range(2):
                rng = slice(32 * h_to + 16 * half, 32 * h_to + 16 * half + 16)
                for h in range(HEADS_HERE):
                    t_a[half, h_to, :, h * HD:(h + 1) * HD] = mixed[h][rng]
                t_a[half, h_to, :, LANES:] = stats[rng]

    with jax.named_scope("text_partial"):
        text_partial()
    text_a = copy_to(t_a.at[1 - c], t_ar, ta_sem.at[0], ta_sem.at[1], sib)
    go(text_a)

    def merge(parts):
        parts = [p.astype(F32) for p in parts]
        out_tops, out_totals, out_mixed = [], [], []
        for h in range(HEADS_HERE):
            tops_h = [p[:, LANES + h:LANES + h + 1] for p in parts]
            top = tops_h[0]
            for other in tops_h[1:]:
                top = jnp.maximum(top, other)
            total, mix = 0.0, 0.0
            for p, top_p in zip(parts, tops_h):
                weight = jnp.exp2((top_p - top) * FACTOR)
                total_p = p[:, LANES + 3 + h:LANES + 4 + h] + p[:, LANES + 6 + h:LANES + 7 + h]
                total = total + total_p * weight
                mix = mix + p[:, h * HD:(h + 1) * HD] * weight
            out_tops.append(top)
            out_totals.append(total)
            out_mixed.append(mix)
        return out_tops, out_totals, out_mixed

    def merged(parts):
        out_tops, out_totals, out_mixed = merge(parts)
        return jnp.concatenate(out_mixed + [pack_stats(out_tops, out_totals)], axis=1)

    def slots_of_window():
        mid = c != xo
        pick_same = mid & (band_ref[0] == xo)
        return (0, jnp.where(mid, 3, 1), jnp.where(pick_same, 1, 2))

    def group_scores(g, with_text):
        slots = slots_of_window()
        for h in range(HEADS_HERE):
            cols = slice(h * HD, (h + 1) * HD)
            query = vq[:, cols]
            scores = [dot_nt(query, kv_of[0][g][s, :, cols]) for s in slots]
            if with_text:
                scores.append(dot_nt(query, tk[:, cols]) + text_bias)
            top = scores[0]
            for score in scores[1:]:
                top = jnp.maximum(top, score)
            top = jnp.max(top, axis=1, keepdims=True)
            base = top * FACTOR
            for i, score in enumerate(scores):
                weights_ref[g, h, i] = jnp.exp2(score * FACTOR - base).astype(BF)
            state_m[g, h] = jnp.broadcast_to(top, (256, HD))

    def group_values(g, with_text):
        slots = slots_of_window()
        for h in range(HEADS_HERE):
            cols = slice(h * HD, (h + 1) * HD)
            total = dot_nn(weights_ref[g, h, 0], with_ones(kv_of[1][g][slots[0], :, cols]))
            for i in (1, 2):
                total = total + dot_nn(weights_ref[g, h, i], with_ones(kv_of[1][g][slots[i], :, cols]))
            if with_text:
                total = total + dot_nn(weights_ref[g, h, 3], with_ones(tv[:, cols]))
            state_o[g, h] = total

    def join_groups():
        for h in range(HEADS_HERE):
            tops = [state_m[g, h] for g in range(3)]
            top = jnp.maximum(jnp.maximum(tops[0], tops[1]), tops[2])
            mix, total = 0.0, 0.0
            for g in range(3):
                factor = jnp.exp2((tops[g] - top) * FACTOR)
                mix = mix + state_o[g, h, :, :HD] * factor
                total = total + state_o[g, h, :, HD:] * factor
            attn[:, :, :, h * HD:(h + 1) * HD] = (mix / total).astype(BF).reshape(2, 4, 32, HD)

    def serve_inter(t, j):
        to_inter(t, j).wait_recv()
        to_sib(INTER, t, j).start()
        if (t, j) in OPP_BY_MATE:
            to_opp(t, j).start()

    def serve_mate(t, j):
        to_mate(t, j).wait_recv()
        if (t, j) in FAR:
            @pl.when(v_recv)
            def _():
                to_far(1, t, j).start()

        to_sib(MATE, t, j).start()
        if (t, j) not in OPP_BY_MATE:
            to_opp(t, j).start()

    def pass_own(t, j):
        @pl.when(v_send)
        def _():
            to_far(0, t, j).wait_recv()
            to_relayed(0, t, j).start()

    def pass_mate(t, j):
        @pl.when(v_send)
        def _():
            to_far(1, t, j).wait_recv()
            to_relayed(1, t, j).start()

    def serve_far(t, j):
        @pl.when(v_recv)
        def _():
            to_relayed(0, t, j).wait_recv()
            to_sib(VERT, t, j).start()
            to_relayed(1, t, j).wait_recv()
            to_sib(VMATE, t, j).start()

    def send_vert(t, j):
        @pl.when(v_send)
        def _():
            to_vert(t, j).start()

    def text_step_a():
        text_a.wait_recv()
        for h_to in range(8):
            t_b[h_to // 4, h_to % 4] = merged([t_a[c, h_to], t_ar[h_to]]).astype(BF)
        copy = copy_to(t_b.at[1 - xr], t_br, ta_sem.at[2], ta_sem.at[3], inter)
        go(copy)
        return copy

    def text_step_b(copy):
        copy.wait_recv()
        for k in range(4):
            t_c[k // 2, k % 2] = merged([t_b[xr, k], t_br[k]]).astype(BF)
        copy = copy_to(t_c.at[1 - xo], t_cr, ta_sem.at[4], ta_sem.at[5], mate)
        go(copy)
        return copy

    def text_step_c(copy):
        copy.wait_recv()
        for k in range(2):
            t_z[k] = merged([t_c[xo, k], t_cr[k]]).astype(BF)
        for dz in range(1, 4):
            copy_to(t_z, t_zr.at[dz], tz_sem.at[0], tz_sem.at[1], at((zh + dz) % 4, x, c)).start()

    def text_step_z():
        block = t_zr.at[pl.ds(1, 3)]
        copy_to(block, block, tz_sem.at[0], tz_sem.at[1], sib).wait_recv()
        for k in range(2):
            _, sums, mix = merge([t_z[k], t_zr[1, k], t_zr[2, k], t_zr[3, k]])
            for h in range(HEADS_HERE):
                t_rows[x, k, :, h * HD:(h + 1) * HD] = (mix[h] / sums[h]).astype(BF)
        for dx in range(1, 4):
            copy_to(t_rows.at[x], t_rows.at[x], tg_sem.at[0], tg_sem.at[1], at(zh, (x + dx) % 4, c)).start()

    def text_gather():
        block = t_rows.at[pl.ds(0, 3)]
        copy_to(block, block, tg_sem.at[0], tg_sem.at[1], sib).wait_recv()
        load_tproj.wait()
        rows_all = t_rows[...].reshape(128, LANES)
        product = dot_nn(rows_all, tproj[...]).astype(BF)
        for k in range(8):
            t_sums[k] = product[16 * k:16 * k + 16]
        for k, (a, b) in enumerate(head_partners):
            copy_to(t_sums.at[a * 4 + b], t_sumr.at[k], ts_sem.at[0], ts_sem.at[1], at_head(a, b)).start()

    def text_sum():
        copy_to(t_sumr, t_sumr, ts_sem.at[0], ts_sem.at[1], sib).wait_recv()
        total = t_sums[head].astype(F32)
        for k in range(7):
            total = total + t_sumr[k].astype(F32)
        t_out[c, x] = total.astype(BF)
        for dx in range(1, 4):
            block = t_out.at[c, x]
            copy_to(block, block, to_sem.at[0], to_sem.at[1], at(zh, (x + dx) % 4, c)).start()

    def text_spread_sib():
        block = t_out.at[c, pl.ds(0, 3)]
        copy_to(block, block, to_sem.at[0], to_sem.at[1], sib).wait_recv()
        go(copy_to(t_out.at[c], t_out.at[c], to_sem.at[2], to_sem.at[3], sib))

    def text_finish():
        block = t_out.at[1 - c]
        copy_to(block, block, to_sem.at[2], to_sem.at[3], sib).wait_recv()
        for cc in range(2):
            for k in range(4):
                tout_ref[16 * cc:16 * cc + 16, k * 768:(k + 1) * 768] = t_out[cc, k].astype(F32)

    def serve_vert(t, j):
        @pl.when(v_recv)
        def _():
            to_vert(t, j).wait_recv()
            to_vmate(t, j).start()
            to_sib(VERT, t, j).start()

    def serve_vmate(t, j):
        @pl.when(v_recv)
        def _():
            to_vmate(t, j).wait_recv()
            to_sib(VMATE, t, j).start()

    def wait_sib(roles, t):
        for role in roles:
            block = kv_of[t][(2 * role + 1) // 4].at[(2 * role + 1) % 4]
            copy_to(block, block, kv_send.at[0], sib_recv.at[role, t], sib).wait_recv()

    def wait_sib_vert(t):
        @pl.when(v_recv)
        def _():
            wait_sib((VERT, VMATE), t)

    def serve_opp(t, j):
        to_opp(t, j).wait_recv()
        to_sib(OPP, t, j).start()

    scope = jax.named_scope
    def many(step, todo):
        with scope(step.__name__):
            for p in todo:
                step(*p)

    def part_of(todo, lo, hi):
        return todo[lo * CHUNKS // 4:hi * CHUNKS // 4]

    def first_hop(lo, hi):
        for k in range(lo * PER, hi * PER):
            many(serve_inter, [order_inter[k]])
            if order_inter[k] not in FAR:
                many(send_vert, [order_inter[k]])
            many(serve_mate, [order_mate[k]])

    first_hop(0, 1)
    with scope("text_sibling_merge"):
        text_copy = text_step_a()
        send_own(order_inter[CHUNKS:], order_mate[CHUNKS:])
    first_hop(1, 4)
    with scope("text_inter_merge"):
        text_copy = text_step_b(text_copy)
    first_hop(4, 6)
    many(pass_own, FAR)
    with scope("text_mate_merge"):
        text_step_c(text_copy)
    first_hop(6, 8)
    many(pass_mate, FAR)
    many(serve_vert, k0 + k1)
    many(serve_vert, k2)
    many(serve_opp, k0 + k1)
    many(serve_vert, k3)
    with scope("wait_own_frame"):
        load_q.wait()
        wait_sib((OWN, MATE), 0)
        wait_sib((OWN, MATE), 1)
    with scope("own_frame"):
        group_scores(0, True)
        group_values(0, True)
    many(serve_vert, v0)
    many(serve_opp, k2 + k3)
    many(serve_vmate, k0 + k1 + k2)
    with scope("projection_halves"):
        for pair in range(2):
            to_pair(pair).wait_recv()
            pair_to_sib(pair).start()
    many(serve_vert, v1)
    with scope("wait_beside_keys"):
        wait_sib((OPP, INTER), 0)
    with scope("frame_beside_scores"):
        group_scores(1, False)
    many(serve_vmate, k3)
    many(serve_opp, v0 + v1 + v2 + v3)
    with scope("text_z_merge"):
        text_step_z()
    many(serve_far, FAR)
    with scope("wait_across_keys"):
        wait_sib_vert(0)
    with scope("frame_across_scores"):
        @pl.when(v_recv)
        def _():
            group_scores(2, False)

        @pl.when(jnp.logical_not(v_recv))
        def _():
            state_m[2] = jnp.full((HEADS_HERE, 256, HD), DEAD, F32)
            state_o[2] = jnp.zeros((HEADS_HERE, 256, 2 * HD), F32)
    many(serve_vmate, v0)
    with scope("wait_beside_values"):
        wait_sib((OPP, INTER), 1)
    with scope("frame_beside_values"):
        group_values(1, False)
    many(serve_vmate, v1)
    with scope("wait_across_values"):
        wait_sib_vert(1)
    with scope("frame_across_values"):
        @pl.when(v_recv)
        def _():
            group_values(2, False)
    with scope("join_groups"):
        join_groups()
    swap_own, swap_pair = [attn.at[:, y_of[0]], attn.at[:, y_of[1]]], attn.at[:, y_opp]
    for pair in range(2):
        copy_to(swap_own[pair], swap_in.at[pair, 0], swap_sem.at[0], swap_sem.at[1 + pair], y_pair[pair]).start()
        copy_to(swap_pair, swap_in.at[pair, 1], swap_sem.at[0], swap_sem.at[1 + pair], y_pair[pair]).start()

    def own_rows(pair):
        return jnp.concatenate(
            [attn[:, y].reshape(64, LANES), attn[:, y_of[1 - pair]].reshape(64, LANES)], axis=0
        )

    with scope("project_own"):
        load_vproj.wait()
        for pair in range(2):
            rows_here = own_rows(pair)
            for q in range(2):
                lo = (2 * pair + q) * PART
                product = dot_nn(rows_here, vproj[:, lo:lo + PART])
                keep[pair, 2 * q], keep[pair, 2 * q + 1] = product[:, :HALF], product[:, HALF:]
        copy_to(wpair.at[0], wpair.at[0], w_sem.at[3], w_sem.at[4], sib).wait_recv()
    with scope("text_gather"):
        text_gather()
    parts_of = [(pair, q) for q in range(4) for pair in range(2)]
    for pair in range(2):
        with scope("swap_wait"):
            copy_to(swap_in.at[pair], swap_in.at[pair], swap_sem.at[0], swap_sem.at[1 + pair], sib).wait_recv()
    for pair, q in parts_of:
        if q % 2 == 0:
            with scope("project_pair"):
                product = dot_nn(swap_in[pair].reshape(128, LANES), wpair[pair, q // 2])
                for k in range(2):
                    total = keep[pair, q + k] + product[:, k * HALF:(k + 1) * HALF]
                    y_out[pair, q + k] = total[64:].astype(BF)
                    keep[pair, q + k, :64] = total[:64]
                    copy_to(
                        y_out.at[pair, q + k], y_in.at[pair, q + k], y_send.at[0], y_recv.at[pair, q + k],
                        y_pair[1 - pair],
                    ).start()
    with scope("text_sum"):
        text_sum()
    for pair, q in parts_of:
        with scope("y_wait"):
            came = y_in.at[pair, q]
            copy_to(came, came, y_send.at[0], y_recv.at[pair, q], sib).wait_recv()
        with scope("y_sum"):
            lo = (4 * pair + q) * HALF
            total = keep[pair, q, :64] + y_in[pair, q].astype(F32)
            vout_ref[:, lo:lo + HALF] = jnp.where(zl == 0, total[:32], total[32:])
            z_out[pair, q] = jnp.where(zl == 0, total[32:], total[:32]).astype(BF)
        copy_to(z_out.at[pair, q], z_in.at[pair, q], z_send.at[0], z_recv.at[pair, q], z_pair).start()
    with scope("text_spread_sib"):
        text_spread_sib()
    for pair, q in parts_of:
        with scope("z_wait"):
            came = z_in.at[pair, q]
            copy_to(came, came, z_send.at[0], z_recv.at[pair, q], sib).wait_recv()
        lo = (4 * pair + q) * HALF
        vout_ref[:, lo:lo + HALF] = vout_ref[:, lo:lo + HALF] + z_in[pair, q].astype(F32)

    with scope("text_finish"):
        text_finish()
    with scope("wait_sends"):
        for copy in sends:
            copy.wait_send()

        whole = k_a.at[pl.ds(0, 2)]
        for kind in (0, 1, 2, 5 + OWN, 5 + MATE, 5 + OPP, 5 + INTER):
            wait_bytes(whole, kv_send.at[kind])

        most, fourth = k_a.at[pl.ds(0, 3), pl.ds(0, 128)], k_a.at[0, pl.ds(0, 128)]

        @pl.when(v_send)
        def _():
            wait_bytes(most, kv_send.at[3])
            wait_bytes(fourth, kv_send.at[13])
            wait_bytes(fourth, kv_send.at[14])

        @pl.when(v_recv)
        def _():
            wait_bytes(most, kv_send.at[4])
            wait_bytes(whole, kv_send.at[5 + VERT])
            wait_bytes(whole, kv_send.at[5 + VMATE])
            wait_bytes(fourth, kv_send.at[11])
            wait_bytes(fourth, kv_send.at[12])

        wait_bytes(t_zr.at[pl.ds(1, 3)], tz_sem.at[0])
        wait_bytes(t_rows.at[pl.ds(0, 3)], tg_sem.at[0])
        wait_bytes(t_sumr, ts_sem.at[0])
        wait_bytes(t_out.at[0, pl.ds(0, 3)], to_sem.at[0])
        wait_bytes(wpair.at[0], w_sem.at[0])
        wait_bytes(wpair.at[0], w_sem.at[3])
        wait_bytes(swap_in, swap_sem.at[0])
        wait_bytes(y_in, y_send.at[0])
        wait_bytes(z_in, z_send.at[0])


def store(video, text, video_out, text_out, sems):
    copies = [
        pltpu.make_async_copy(video, video_out, sems.at[0]),
        pltpu.make_async_copy(text, text_out, sems.at[1]),
    ]
    for copy in copies:
        copy.start()
    for copy in copies:
        copy.wait()


def body(video_q, video_k, video_v, text_q, text_k, text_v, band_start, text_mask, video_proj, text_proj):
    dma = pltpu.SemaphoreType.DMA
    vmem = pltpu.VMEM
    hbm_spec = pl.BlockSpec(memory_space=pltpu.HBM)
    vmem_spec = pl.BlockSpec(memory_space=pltpu.VMEM)
    outs = pl.pallas_call(
        kernel,
        name="joint_attention",
        out_shape=(pltpu.VMEM((32, WIDTH), F32), pltpu.VMEM((32, WIDTH), F32)),
        in_specs=[hbm_spec] * 10,
        out_specs=(vmem_spec, vmem_spec),
        scratch_shapes=[
            pltpu.SMEM((1,), jnp.int32),
            vmem((1, TXT), jnp.int32),
            *[vmem((4, 256, LANES), BF) for _ in range(6)],
            vmem((256, LANES), BF),
            vmem((256, LANES), BF),
            vmem((256, LANES), BF),
            vmem((256, LANES), BF),
            vmem((LANES, WIDTH), BF),
            vmem((LANES, 768), BF),
            vmem((3, HEADS_HERE, 256, 2 * HD), F32),
            vmem((3, HEADS_HERE, 256, HD), F32),
            vmem((3, HEADS_HERE, 4, 256, 256), BF),
            vmem((2, 4, 32, LANES), BF),
            vmem((2, 2, LANES, PART), BF),
            vmem((2, len(FAR), 256 // CHUNKS, LANES), BF),
            dma((15,)),
            dma((6, 2, CHUNKS)),
            dma((6, 2)),
            dma((2, len(FAR))),
            dma((10,)),
            vmem((2, 8, 16, 512), BF),
            vmem((8, 16, 512), BF),
            vmem((2, 4, 16, 512), BF),
            vmem((4, 16, 512), BF),
            vmem((2, 2, 16, 512), BF),
            vmem((2, 16, 512), BF),
            vmem((2, 16, 512), BF),
            vmem((4, 2, 16, 512), BF),
            vmem((4, 2, 16, LANES), BF),
            vmem((8, 16, 768), BF),
            vmem((7, 16, 768), BF),
            vmem((2, 4, 16, 768), BF),
            dma((6,)),
            dma((2,)),
            dma((2,)),
            dma((2,)),
            dma((4,)),
            vmem((2, 2, 2, 32, LANES), BF),
            vmem((2, 4, 128, HALF), F32),
            vmem((2, 4, 64, HALF), BF),
            vmem((2, 4, 64, HALF), BF),
            vmem((2, 4, 32, HALF), BF),
            vmem((2, 4, 32, HALF), BF),
            dma((5,)),
            dma((3,)),
            dma((1,)),
            dma((2, 4)),
            dma((1,)),
            dma((2, 4)),
        ],
        compiler_params=pltpu.CompilerParams(
            collective_id=0, has_side_effects=True, vmem_limit_bytes=56 * 2**20
        ),
        cost_estimate=pl.CostEstimate(flops=2_000_000_000, bytes_accessed=8_000_000, transcendentals=2_500_000),
    )(
        video_q, video_k, video_v, text_q, text_k, text_v, band_start, text_mask.reshape(1, TXT),
        video_proj, text_proj,
    )
    result = jax.ShapeDtypeStruct((32, WIDTH), F32)
    return pl.pallas_call(
        store,
        name="store",
        out_shape=(result, result),
        in_specs=[vmem_spec, vmem_spec],
        out_specs=(hbm_spec, hbm_spec),
        scratch_shapes=[dma((2,))],
    )(*[pltpu.with_memory_space_constraint(out, pltpu.VMEM) for out in outs])


def solution(mesh):
    return jax.shard_map(
        body,
        mesh=mesh,
        in_specs=(
            P("frm", "head"), P("frm", "head"), P("frm", "head"),
            P(None, "head"), P(None, "head"), P(None, "head"),
            P("frm"), P(), P("head", None), P("head", None),
        ),
        out_specs=(P(("frm", "head"), None), P("head", None)),
        check_vma=False,
    )
```

```python
import math

import jax
import jax.numpy as jnp
from jax import lax
from jax.experimental import pallas as pl
from jax.experimental.pallas import tpu as pltpu
from jax.sharding import PartitionSpec as P

HD = 128
TXT = 256
BANDS = 4
HEADS_HERE = 3
LANES = HEADS_HERE * HD
WIDTH = 3072
MESH = pl.DeviceIdType.MESH
BF = jnp.bfloat16
F32 = jnp.float32
FACTOR = math.log2(math.e) / math.sqrt(HD)
DEAD = -1e30
CHUNKS = 4
OWN, MATE, OPP, INTER, VMATE, VERT = range(6)
PER = CHUNKS // 4


def quarter(t, k):
    return tuple((t, k * PER + i) for i in range(PER))


FAR = quarter(1, 2) + quarter(1, 3)
OPP_BY_MATE = quarter(1, 0) + quarter(1, 1) + quarter(1, 2)
PART = 768
HALF = PART // 2


def dot_nt(a, b):
    return lax.dot_general(a, b, (((1,), (1,)), ((), ())), preferred_element_type=F32)


def dot_nn(a, b):
    return jnp.dot(a, b, preferred_element_type=F32)


def with_ones(values):
    return jnp.concatenate([values, jnp.ones(values.shape, BF)], axis=1)


def kernel(
    vq_hbm, vk_hbm, vv_hbm, tq_hbm, tk_hbm, tv_hbm, band_hbm, mask_hbm, vproj_hbm, tproj_hbm,
    vout_ref, tout_ref,
    band_ref, mask_ref, k_a, k_b, k_c, v_a, v_b, v_c, vq, tq, tk, tv, vproj, tproj, state_o, state_m, weights_ref, attn, wpair, relay,
    kv_send, kv_recv, sib_recv, relay_recv, load_sem,
    t_a, t_ar, t_b, t_br, t_c, t_cr, t_zr, t_rows, t_sums, t_sumr, t_out,
    ta_sem, tz_sem, tg_sem, ts_sem, to_sem,
    swap_in, keep, y_out, y_in, z_out, z_in,
    w_sem, swap_sem, y_send, y_recv, z_send, z_recv,
):
    frm = lax.axis_index("frm")
    head = lax.axis_index("head")
    zh, x, c = frm // 8, (frm // 2) % 4, frm % 2
    zl, y = head // 4, head % 4
    xr, xo = x // 2, x % 2

    def at(zh_, x_, c_):
        return {"frm": zh_ * 8 + x_ * 2 + c_, "head": head}

    def at_head(zl_, y_):
        return {"frm": frm, "head": zl_ * 4 + y_}

    x_mate = x + 1 - 2 * xo
    sib = at(zh, x, 1 - c)
    mate = at(zh, x_mate, c)
    inter = at(zh, 3 - x, c)
    z_pair = at_head(1 - zl, y)
    y_of = (y + 1 - 2 * (y % 2), 3 - y)
    y_opp = (y + 2) % 4
    y_pair = (at_head(zl, y_of[0]), at_head(zl, y_of[1]))
    zh_to = zh + 1 - 2 * xr
    v_send = (zh_to >= 0) & (zh_to <= 3)
    zh_from = zh - 1 + 2 * xr
    v_recv = (zh_from >= 0) & (zh_from <= 3)
    vert = at(jnp.clip(zh_to, 0, 3), x, c)
    far = at(jnp.clip(zh_from, 0, 3), x, c)

    def copy_to(src, dst, send, recv, device):
        return pltpu.make_async_remote_copy(
            src_ref=src, dst_ref=dst, send_sem=send, recv_sem=recv,
            device_id=device, device_id_type=MESH,
        )

    loads = []

    def load(src, dst):
        copy = pltpu.make_async_copy(src, dst, load_sem.at[len(loads)])
        copy.start()
        loads.append(copy)
        return copy

    load_own = [load(vk_hbm, k_a.at[0]), load(vv_hbm, v_a.at[0])]
    load_text = [
        load(tq_hbm, tq), load(tk_hbm, tk), load(tv_hbm, tv), load(mask_hbm, mask_ref), load(band_hbm, band_ref)
    ]
    load_q = load(vq_hbm, vq)
    load_vproj = load(vproj_hbm, vproj)
    load_tproj = load(tproj_hbm.at[:, pl.ds(pl.multiple_of(x * 768, 768), 768)], tproj)

    frm_partners = [sib]
    frm_partners += [at((zh + d) % 4, x, c) for d in range(1, 4)]
    frm_partners += [at(zh, (x + d) % 4, c) for d in range(1, 4)]
    head_partners = [
        ((zl + dz) % 2, (y + dy) % 4) for dz in range(2) for dy in range(4) if (dz, dy) != (0, 0)
    ]
    barrier = pltpu.get_barrier_semaphore()
    with jax.named_scope("barrier"):
        for device in frm_partners + [at_head(a, b) for a, b in head_partners]:
            pl.semaphore_signal(barrier, inc=1, device_id=device, device_id_type=MESH)
        pl.semaphore_wait(barrier, len(frm_partners) + len(head_partners))

    rows = 256 // CHUNKS
    sends = []

    def kv_copy(kind, t, j, src_slot, dst_slot, device, src=None):
        rng = pl.ds(j * rows, rows)
        return copy_to(
            kv_of[t][src_slot // 4].at[src_slot % 4, rng] if src is None else src.at[rng],
            kv_of[t][dst_slot // 4].at[dst_slot % 4, rng],
            kv_send.at[kind],
            sib_recv.at[dst_slot // 2, t] if dst_slot % 2 else kv_recv.at[dst_slot // 2, t, j],
            device,
        )

    kv_of = ((k_a, k_b, k_c), (v_a, v_b, v_c))
    pieces = [(t, j) for t in range(2) for j in range(CHUNKS)]
    own_hbm = (vk_hbm, vv_hbm)

    def to_mate(t, j):
        return kv_copy(0, t, j, 0, 2 * MATE, mate, own_hbm[t])

    def to_inter(t, j):
        return kv_copy(1, t, j, 0, 2 * INTER, inter, own_hbm[t])

    def to_opp(t, j):
        if (t, j) in OPP_BY_MATE:
            return kv_copy(2, t, j, 2 * INTER, 2 * OPP, mate)
        return kv_copy(2, t, j, 2 * MATE, 2 * OPP, inter)

    def to_far(which, t, j):
        k = FAR.index((t, j))
        rng = pl.ds(j * rows, rows)
        return copy_to(
            own_hbm[t].at[rng] if which == 0 else kv_of[t][0].at[2 * MATE, rng],
            relay.at[which, k], kv_send.at[11 + which], relay_recv.at[which, k], far,
        )

    def to_relayed(which, t, j):
        k = FAR.index((t, j))
        role = (VERT, VMATE)[which]
        return copy_to(
            relay.at[which, k], kv_of[t][2].at[2 * role % 4, pl.ds(j * rows, rows)],
            kv_send.at[13 + which], kv_recv.at[role, t, j], inter,
        )

    def to_vert(t, j):
        return kv_copy(3, t, j, 2 * INTER, 2 * VERT, vert)

    def to_vmate(t, j):
        return kv_copy(4, t, j, 2 * VERT, 2 * VMATE, mate)

    def to_sib(role, t, j):
        return kv_copy(5 + role, t, j, 2 * role, 2 * role + 1, sib, own_hbm[t] if role == OWN else None)

    def go(copy):
        copy.start()
        sends.append(copy)

    def wait_bytes(ref, sem):
        copy_to(ref, ref, sem, kv_recv.at[0, 0, 0], sib).wait_send()

    def send_own(todo_inter, todo_mate):
        for p_inter, p_mate in zip(todo_inter, todo_mate):
            to_inter(*p_inter).start()
            to_mate(*p_mate).start()
            to_sib(OWN, *p_mate).start()

    (k0, k1, k2, k3), (v0, v1, v2, v3) = [[quarter(t, k) for k in range(4)] for t in range(2)]
    order_inter = k0 + k1 + k2 + k3 + v0 + v1 + v2 + v3
    order_mate = k0 + k1 + v2 + v3 + k2 + k3 + v0 + v1
    send_own(order_inter[:CHUNKS], order_mate[:CHUNKS])

    @pl.when(v_recv)
    def _():
        for t, j in FAR:
            to_far(0, t, j).start()

    def to_pair(pair):
        cols = pl.ds(pl.multiple_of(2 * PART * pair + PART * c, PART), PART)
        return copy_to(vproj_hbm.at[:, cols], wpair.at[pair, c], w_sem.at[0], w_sem.at[1 + pair], y_pair[pair])

    def pair_to_sib(pair):
        return copy_to(wpair.at[pair, c], wpair.at[pair, c], w_sem.at[3], w_sem.at[4], sib)

    for pair in range(2):
        to_pair(pair).start()

    for copy in load_own + load_text:
        copy.wait()
    lane = lax.broadcasted_iota(jnp.int32, (1, TXT), 1)
    text_bias = jnp.where(mask_ref[...] == 1, 0.0, DEAD)
    first_bias = jnp.where(frm == 0, text_bias, DEAD)

    def pack_stats(tops, totals):
        count = tops[0].shape[0]
        at_lane = lax.broadcasted_iota(jnp.int32, (count, HD), 1)
        packed = jnp.zeros((count, HD), F32)
        for h in range(HEADS_HERE):
            high = totals[h].astype(BF).astype(F32)
            packed = jnp.where(at_lane == h, tops[h], packed)
            packed = jnp.where(at_lane == 3 + h, high, packed)
            packed = jnp.where(at_lane == 6 + h, totals[h] - high, packed)
        return packed

    def text_partial():
        tops, totals, mixed = [], [], []
        for h in range(HEADS_HERE):
            cols = slice(h * HD, (h + 1) * HD)
            s_own = dot_nt(tq[:, cols], k_a[0, :, cols])
            s_text = dot_nt(tq[:, cols], tk[:, cols]) + first_bias
            top = jnp.maximum(
                jnp.max(s_own, axis=1, keepdims=True), jnp.max(s_text, axis=1, keepdims=True)
            ).astype(BF).astype(F32)
            base = top * FACTOR
            w_own = jnp.exp2(s_own * FACTOR - base).astype(BF)
            w_text = jnp.exp2(s_text * FACTOR - base).astype(BF)
            both = dot_nn(w_own, with_ones(v_a[0, :, cols])) + dot_nn(w_text, with_ones(tv[:, cols]))
            tops.append(top)
            totals.append(both[:, HD:HD + 1])
            mixed.append(both[:, :HD].astype(BF))
        stats = pack_stats(tops, totals).astype(BF)
        for h_to in range(8):
            for half in range(2):
                rng = slice(32 * h_to + 16 * half, 32 * h_to + 16 * half + 16)
                for h in range(HEADS_HERE):
                    t_a[half, h_to, :, h * HD:(h + 1) * HD] = mixed[h][rng]
                t_a[half, h_to, :, LANES:] = stats[rng]

    with jax.named_scope("text_partial"):
        text_partial()
    text_a = copy_to(t_a.at[1 - c], t_ar, ta_sem.at[0], ta_sem.at[1], sib)
    go(text_a)

    def merge(parts):
        parts = [p.astype(F32) for p in parts]
        out_tops, out_totals, out_mixed = [], [], []
        for h in range(HEADS_HERE):
            tops_h = [p[:, LANES + h:LANES + h + 1] for p in parts]
            top = tops_h[0]
            for other in tops_h[1:]:
                top = jnp.maximum(top, other)
            total, mix = 0.0, 0.0
            for p, top_p in zip(parts, tops_h):
                weight = jnp.exp2((top_p - top) * FACTOR)
                total_p = p[:, LANES + 3 + h:LANES + 4 + h] + p[:, LANES + 6 + h:LANES + 7 + h]
                total = total + total_p * weight
                mix = mix + p[:, h * HD:(h + 1) * HD] * weight
            out_tops.append(top)
            out_totals.append(total)
            out_mixed.append(mix)
        return out_tops, out_totals, out_mixed

    def merged(parts):
        out_tops, out_totals, out_mixed = merge(parts)
        return jnp.concatenate(out_mixed + [pack_stats(out_tops, out_totals)], axis=1)

    def slots_of_window():
        mid = c != xo
        pick_same = mid & (band_ref[0] == xo)
        return (0, jnp.where(mid, 3, 1), jnp.where(pick_same, 1, 2))

    def group_scores(g, with_text):
        slots = slots_of_window()
        for h in range(HEADS_HERE):
            cols = slice(h * HD, (h + 1) * HD)
            query = vq[:, cols]
            scores = [dot_nt(query, kv_of[0][g][s, :, cols]) for s in slots]
            if with_text:
                scores.append(dot_nt(query, tk[:, cols]) + text_bias)
            top = scores[0]
            for score in scores[1:]:
                top = jnp.maximum(top, score)
            top = jnp.max(top, axis=1, keepdims=True)
            base = top * FACTOR
            for i, score in enumerate(scores):
                weights_ref[g, h, i] = jnp.exp2(score * FACTOR - base).astype(BF)
            state_m[g, h] = jnp.broadcast_to(top, (256, HD))

    def group_values(g, with_text):
        slots = slots_of_window()
        for h in range(HEADS_HERE):
            cols = slice(h * HD, (h + 1) * HD)
            total = dot_nn(weights_ref[g, h, 0], with_ones(kv_of[1][g][slots[0], :, cols]))
            for i in (1, 2):
                total = total + dot_nn(weights_ref[g, h, i], with_ones(kv_of[1][g][slots[i], :, cols]))
            if with_text:
                total = total + dot_nn(weights_ref[g, h, 3], with_ones(tv[:, cols]))
            state_o[g, h] = total

    def join_groups():
        for h in range(HEADS_HERE):
            tops = [state_m[g, h] for g in range(3)]
            top = jnp.maximum(jnp.maximum(tops[0], tops[1]), tops[2])
            mix, total = 0.0, 0.0
            for g in range(3):
                factor = jnp.exp2((tops[g] - top) * FACTOR)
                mix = mix + state_o[g, h, :, :HD] * factor
                total = total + state_o[g, h, :, HD:] * factor
            attn[:, :, :, h * HD:(h + 1) * HD] = (mix / total).astype(BF).reshape(2, 4, 32, HD)

    def serve_inter(t, j):
        to_inter(t, j).wait_recv()
        to_sib(INTER, t, j).start()
        if (t, j) in OPP_BY_MATE:
            to_opp(t, j).start()

    def serve_mate(t, j):
        to_mate(t, j).wait_recv()
        if (t, j) in FAR:
            @pl.when(v_recv)
            def _():
                to_far(1, t, j).start()

        to_sib(MATE, t, j).start()
        if (t, j) not in OPP_BY_MATE:
            to_opp(t, j).start()

    def pass_own(t, j):
        @pl.when(v_send)
        def _():
            to_far(0, t, j).wait_recv()
            to_relayed(0, t, j).start()

    def pass_mate(t, j):
        @pl.when(v_send)
        def _():
            to_far(1, t, j).wait_recv()
            to_relayed(1, t, j).start()

    def serve_far(t, j):
        @pl.when(v_recv)
        def _():
            to_relayed(0, t, j).wait_recv()
            to_sib(VERT, t, j).start()
            to_relayed(1, t, j).wait_recv()
            to_sib(VMATE, t, j).start()

    def send_vert(t, j):
        @pl.when(v_send)
        def _():
            to_vert(t, j).start()

    def text_step_a():
        text_a.wait_recv()
        for h_to in range(8):
            t_b[h_to // 4, h_to % 4] = merged([t_a[c, h_to], t_ar[h_to]]).astype(BF)
        copy = copy_to(t_b.at[1 - xr], t_br, ta_sem.at[2], ta_sem.at[3], inter)
        go(copy)
        return copy

    def text_step_b(copy):
        copy.wait_recv()
        for k in range(4):
            t_c[k // 2, k % 2] = merged([t_b[xr, k], t_br[k]]).astype(BF)
        copy = copy_to(t_c.at[1 - xo], t_cr, ta_sem.at[4], ta_sem.at[5], mate)
        go(copy)
        return copy

    def text_step_c(copy):
        copy.wait_recv()
        for k in range(2):
            t_zr[zh, k] = merged([t_c[xo, k], t_cr[k]]).astype(BF)
        for dz in range(1, 4):
            copy_to(t_zr.at[zh], t_zr.at[zh], tz_sem.at[0], tz_sem.at[1], at((zh + dz) % 4, x, c)).start()

    def text_step_z():
        block = t_zr.at[pl.ds(1, 3)]
        copy_to(block, block, tz_sem.at[0], tz_sem.at[1], sib).wait_recv()
        for k in range(2):
            _, sums, mix = merge([t_zr[i, k] for i in range(4)])
            for h in range(HEADS_HERE):
                t_rows[x, k, :, h * HD:(h + 1) * HD] = (mix[h] / sums[h]).astype(BF)
        for dx in range(1, 4):
            copy_to(t_rows.at[x], t_rows.at[x], tg_sem.at[0], tg_sem.at[1], at(zh, (x + dx) % 4, c)).start()

    def text_gather():
        block = t_rows.at[pl.ds(0, 3)]
        copy_to(block, block, tg_sem.at[0], tg_sem.at[1], sib).wait_recv()
        load_tproj.wait()
        rows_all = t_rows[...].reshape(128, LANES)
        product = dot_nn(rows_all, tproj[...]).astype(BF)
        for k in range(8):
            t_sums[k] = product[16 * k:16 * k + 16]
        for k, (a, b) in enumerate(head_partners):
            copy_to(t_sums.at[a * 4 + b], t_sumr.at[k], ts_sem.at[0], ts_sem.at[1], at_head(a, b)).start()

    def text_sum():
        copy_to(t_sumr, t_sumr, ts_sem.at[0], ts_sem.at[1], sib).wait_recv()
        total = t_sums[head].astype(F32)
        for k in range(7):
            total = total + t_sumr[k].astype(F32)
        t_out[c, x] = total.astype(BF)
        for dx in range(1, 4):
            block = t_out.at[c, x]
            copy_to(block, block, to_sem.at[0], to_sem.at[1], at(zh, (x + dx) % 4, c)).start()

    def text_spread_sib():
        block = t_out.at[c, pl.ds(0, 3)]
        copy_to(block, block, to_sem.at[0], to_sem.at[1], sib).wait_recv()
        go(copy_to(t_out.at[c], t_out.at[c], to_sem.at[2], to_sem.at[3], sib))

    def text_finish():
        block = t_out.at[1 - c]
        copy_to(block, block, to_sem.at[2], to_sem.at[3], sib).wait_recv()
        for cc in range(2):
            for k in range(4):
                tout_ref[16 * cc:16 * cc + 16, k * 768:(k + 1) * 768] = t_out[cc, k].astype(F32)

    def serve_vert(t, j):
        @pl.when(v_recv)
        def _():
            to_vert(t, j).wait_recv()
            to_vmate(t, j).start()
            to_sib(VERT, t, j).start()

    def serve_vmate(t, j):
        @pl.when(v_recv)
        def _():
            to_vmate(t, j).wait_recv()
            to_sib(VMATE, t, j).start()

    def wait_sib(roles, t):
        for role in roles:
            block = kv_of[t][(2 * role + 1) // 4].at[(2 * role + 1) % 4]
            copy_to(block, block, kv_send.at[0], sib_recv.at[role, t], sib).wait_recv()

    def wait_sib_vert(t):
        @pl.when(v_recv)
        def _():
            wait_sib((VERT, VMATE), t)

    def serve_opp(t, j):
        to_opp(t, j).wait_recv()
        to_sib(OPP, t, j).start()

    scope = jax.named_scope
    def many(step, todo):
        with scope(step.__name__):
            for p in todo:
                step(*p)

    def part_of(todo, lo, hi):
        return todo[lo * CHUNKS // 4:hi * CHUNKS // 4]

    def first_hop(lo, hi):
        for k in range(lo * PER, hi * PER):
            many(serve_inter, [order_inter[k]])
            if order_inter[k] not in FAR:
                many(send_vert, [order_inter[k]])
            many(serve_mate, [order_mate[k]])

    with scope("text_sibling_merge"):
        text_copy = text_step_a()
        send_own(order_inter[CHUNKS:], order_mate[CHUNKS:])
    first_hop(0, 4)
    with scope("text_inter_merge"):
        text_copy = text_step_b(text_copy)
    first_hop(4, 6)
    many(pass_own, FAR)
    with scope("text_mate_merge"):
        text_step_c(text_copy)
    first_hop(6, 8)
    many(pass_mate, FAR)
    many(serve_vert, k0 + k1)
    many(serve_vert, k2)
    many(serve_opp, k0 + k1)
    many(serve_vert, k3)
    with scope("wait_own_frame"):
        load_q.wait()
        wait_sib((OWN, MATE), 0)
        wait_sib((OWN, MATE), 1)
    with scope("own_frame"):
        group_scores(0, True)
        group_values(0, True)
    many(serve_vert, v0)
    many(serve_opp, k2 + k3)
    many(serve_vmate, k0 + k1 + k2)
    with scope("projection_halves"):
        for pair in range(2):
            to_pair(pair).wait_recv()
            pair_to_sib(pair).start()
    many(serve_vert, v1)
    with scope("text_z_merge"):
        text_step_z()
    with scope("wait_beside_keys"):
        wait_sib((OPP, INTER), 0)
    with scope("frame_beside_scores"):
        group_scores(1, False)
    many(serve_vmate, k3)
    many(serve_opp, v0 + v1 + v2 + v3)
    many(serve_far, FAR)
    many(serve_vmate, v0 + v1)
    with scope("text_gather"):
        text_gather()
    with scope("wait_across_keys"):
        wait_sib_vert(0)
    with scope("frame_across_scores"):
        @pl.when(v_recv)
        def _():
            group_scores(2, False)

        @pl.when(jnp.logical_not(v_recv))
        def _():
            state_m[2] = jnp.full((HEADS_HERE, 256, HD), DEAD, F32)
            state_o[2] = jnp.zeros((HEADS_HERE, 256, 2 * HD), F32)
    with scope("wait_beside_values"):
        wait_sib((OPP, INTER), 1)
    with scope("frame_beside_values"):
        group_values(1, False)
    with scope("wait_across_values"):
        wait_sib_vert(1)
    with scope("frame_across_values"):
        @pl.when(v_recv)
        def _():
            group_values(2, False)
    with scope("join_groups"):
        join_groups()
    swap_own, swap_pair = [attn.at[:, y_of[0]], attn.at[:, y_of[1]]], attn.at[:, y_opp]
    for pair in range(2):
        copy_to(swap_own[pair], swap_in.at[pair, 0], swap_sem.at[0], swap_sem.at[1 + pair], y_pair[pair]).start()
        copy_to(swap_pair, swap_in.at[pair, 1], swap_sem.at[0], swap_sem.at[1 + pair], y_pair[pair]).start()

    def own_rows(pair):
        return jnp.concatenate(
            [attn[:, y].reshape(64, LANES), attn[:, y_of[1 - pair]].reshape(64, LANES)], axis=0
        )

    with scope("project_own"):
        load_vproj.wait()
        for pair in range(2):
            rows_here = own_rows(pair)
            for q in range(2):
                lo = (2 * pair + q) * PART
                product = dot_nn(rows_here, vproj[:, lo:lo + PART])
                keep[pair, 2 * q], keep[pair, 2 * q + 1] = product[:, :HALF], product[:, HALF:]
        copy_to(wpair.at[0], wpair.at[0], w_sem.at[3], w_sem.at[4], sib).wait_recv()
    with scope("text_sum"):
        text_sum()
    parts_of = [(pair, q) for q in range(4) for pair in range(2)]
    for pair in range(2):
        with scope("swap_wait"):
            copy_to(swap_in.at[pair], swap_in.at[pair], swap_sem.at[0], swap_sem.at[1 + pair], sib).wait_recv()
    for pair, q in parts_of:
        if q % 2 == 0:
            with scope("project_pair"):
                product = dot_nn(swap_in[pair].reshape(128, LANES), wpair[pair, q // 2])
                for k in range(2):
                    total = keep[pair, q + k] + product[:, k * HALF:(k + 1) * HALF]
                    y_out[pair, q + k] = total[64:].astype(BF)
                    keep[pair, q + k, :64] = total[:64]
                    copy_to(
                        y_out.at[pair, q + k], y_in.at[pair, q + k], y_send.at[0], y_recv.at[pair, q + k],
                        y_pair[1 - pair],
                    ).start()
    with scope("text_spread_sib"):
        text_spread_sib()
    for pair, q in parts_of:
        with scope("y_wait"):
            came = y_in.at[pair, q]
            copy_to(came, came, y_send.at[0], y_recv.at[pair, q], sib).wait_recv()
        with scope("y_sum"):
            lo = (4 * pair + q) * HALF
            total = keep[pair, q, :64] + y_in[pair, q].astype(F32)
            vout_ref[:, lo:lo + HALF] = jnp.where(zl == 0, total[:32], total[32:])
            z_out[pair, q] = jnp.where(zl == 0, total[32:], total[:32]).astype(BF)
        copy_to(z_out.at[pair, q], z_in.at[pair, q], z_send.at[0], z_recv.at[pair, q], z_pair).start()
    for pair, q in parts_of:
        with scope("z_wait"):
            came = z_in.at[pair, q]
            copy_to(came, came, z_send.at[0], z_recv.at[pair, q], sib).wait_recv()
        lo = (4 * pair + q) * HALF
        vout_ref[:, lo:lo + HALF] = vout_ref[:, lo:lo + HALF] + z_in[pair, q].astype(F32)

    with scope("text_finish"):
        text_finish()
    with scope("wait_sends"):
        for copy in sends:
            copy.wait_send()

        whole = k_a.at[pl.ds(0, 2)]
        for kind in (0, 1, 2, 5 + OWN, 5 + MATE, 5 + OPP, 5 + INTER):
            wait_bytes(whole, kv_send.at[kind])

        most, fourth = k_a.at[pl.ds(0, 3), pl.ds(0, 128)], k_a.at[0, pl.ds(0, 128)]

        @pl.when(v_send)
        def _():
            wait_bytes(most, kv_send.at[3])
            wait_bytes(fourth, kv_send.at[13])
            wait_bytes(fourth, kv_send.at[14])

        @pl.when(v_recv)
        def _():
            wait_bytes(most, kv_send.at[4])
            wait_bytes(whole, kv_send.at[5 + VERT])
            wait_bytes(whole, kv_send.at[5 + VMATE])
            wait_bytes(fourth, kv_send.at[11])
            wait_bytes(fourth, kv_send.at[12])

        wait_bytes(t_zr.at[pl.ds(1, 3)], tz_sem.at[0])
        wait_bytes(t_rows.at[pl.ds(0, 3)], tg_sem.at[0])
        wait_bytes(t_sumr, ts_sem.at[0])
        wait_bytes(t_out.at[0, pl.ds(0, 3)], to_sem.at[0])
        wait_bytes(wpair.at[0], w_sem.at[0])
        wait_bytes(wpair.at[0], w_sem.at[3])
        wait_bytes(swap_in, swap_sem.at[0])
        wait_bytes(y_in, y_send.at[0])
        wait_bytes(z_in, z_send.at[0])


def store(video, text, video_out, text_out, sems):
    copies = [
        pltpu.make_async_copy(video, video_out, sems.at[0]),
        pltpu.make_async_copy(text, text_out, sems.at[1]),
    ]
    for copy in copies:
        copy.start()
    for copy in copies:
        copy.wait()


def body(video_q, video_k, video_v, text_q, text_k, text_v, band_start, text_mask, video_proj, text_proj):
    dma = pltpu.SemaphoreType.DMA
    vmem = pltpu.VMEM
    hbm_spec = pl.BlockSpec(memory_space=pltpu.HBM)
    vmem_spec = pl.BlockSpec(memory_space=pltpu.VMEM)
    outs = pl.pallas_call(
        kernel,
        name="joint_attention",
        out_shape=(pltpu.VMEM((32, WIDTH), F32), pltpu.VMEM((32, WIDTH), F32)),
        in_specs=[hbm_spec] * 10,
        out_specs=(vmem_spec, vmem_spec),
        scratch_shapes=[
            pltpu.SMEM((1,), jnp.int32),
            vmem((1, TXT), jnp.int32),
            *[vmem((4, 256, LANES), BF) for _ in range(6)],
            vmem((256, LANES), BF),
            vmem((256, LANES), BF),
            vmem((256, LANES), BF),
            vmem((256, LANES), BF),
            vmem((LANES, WIDTH), BF),
            vmem((LANES, 768), BF),
            vmem((3, HEADS_HERE, 256, 2 * HD), F32),
            vmem((3, HEADS_HERE, 256, HD), F32),
            vmem((3, HEADS_HERE, 4, 256, 256), BF),
            vmem((2, 4, 32, LANES), BF),
            vmem((2, 2, LANES, PART), BF),
            vmem((2, len(FAR), 256 // CHUNKS, LANES), BF),
            dma((15,)),
            dma((6, 2, CHUNKS)),
            dma((6, 2)),
            dma((2, len(FAR))),
            dma((10,)),
            vmem((2, 8, 16, 512), BF),
            vmem((8, 16, 512), BF),
            vmem((2, 4, 16, 512), BF),
            vmem((4, 16, 512), BF),
            vmem((2, 2, 16, 512), BF),
            vmem((2, 16, 512), BF),
            vmem((4, 2, 16, 512), BF),
            vmem((4, 2, 16, LANES), BF),
            vmem((8, 16, 768), BF),
            vmem((7, 16, 768), BF),
            vmem((2, 4, 16, 768), BF),
            dma((6,)),
            dma((2,)),
            dma((2,)),
            dma((2,)),
            dma((4,)),
            vmem((2, 2, 2, 32, LANES), BF),
            vmem((2, 4, 128, HALF), F32),
            vmem((2, 4, 64, HALF), BF),
            vmem((2, 4, 64, HALF), BF),
            vmem((2, 4, 32, HALF), BF),
            vmem((2, 4, 32, HALF), BF),
            dma((5,)),
            dma((3,)),
            dma((1,)),
            dma((2, 4)),
            dma((1,)),
            dma((2, 4)),
        ],
        compiler_params=pltpu.CompilerParams(
            collective_id=0, has_side_effects=True, vmem_limit_bytes=56 * 2**20
        ),
        cost_estimate=pl.CostEstimate(flops=2_000_000_000, bytes_accessed=8_000_000, transcendentals=2_500_000),
    )(
        video_q, video_k, video_v, text_q, text_k, text_v, band_start, text_mask.reshape(1, TXT),
        video_proj, text_proj,
    )
    result = jax.ShapeDtypeStruct((32, WIDTH), F32)
    return pl.pallas_call(
        store,
        name="store",
        out_shape=(result, result),
        in_specs=[vmem_spec, vmem_spec],
        out_specs=(hbm_spec, hbm_spec),
        scratch_shapes=[dma((2,))],
    )(*[pltpu.with_memory_space_constraint(out, pltpu.VMEM) for out in outs])


def solution(mesh):
    return jax.shard_map(
        body,
        mesh=mesh,
        in_specs=(
            P("frm", "head"), P("frm", "head"), P("frm", "head"),
            P(None, "head"), P(None, "head"), P(None, "head"),
            P("frm"), P(), P("head", None), P("head", None),
        ),
        out_specs=(P(("frm", "head"), None), P("head", None)),
        check_vma=False,
    )
```

```python
import math

import jax
import jax.numpy as jnp
from jax import lax
from jax.experimental import pallas as pl
from jax.experimental.pallas import tpu as pltpu
from jax.sharding import PartitionSpec as P

HD = 128
TXT = 256
BANDS = 4
HEADS_HERE = 3
LANES = HEADS_HERE * HD
WIDTH = 3072
MESH = pl.DeviceIdType.MESH
BF = jnp.bfloat16
F32 = jnp.float32
FACTOR = math.log2(math.e) / math.sqrt(HD)
DEAD = -1e30
CHUNKS = 4
OWN, MATE, OPP, INTER, VMATE, VERT = range(6)
PER = CHUNKS // 4


def quarter(t, k):
    return tuple((t, k * PER + i) for i in range(PER))


FAR = quarter(1, 2) + quarter(1, 3)
OPP_BY_MATE = quarter(1, 0) + quarter(1, 1) + quarter(1, 2)
PART = 768
HALF = PART // 2


def dot_nt(a, b):
    return lax.dot_general(a, b, (((1,), (1,)), ((), ())), preferred_element_type=F32)


def dot_nn(a, b):
    return jnp.dot(a, b, preferred_element_type=F32)


def with_ones(values):
    return jnp.concatenate([values, jnp.ones(values.shape, BF)], axis=1)


def kernel(
    vq_hbm, vk_hbm, vv_hbm, tq_hbm, tk_hbm, tv_hbm, band_hbm, mask_hbm, vproj_hbm, tproj_hbm,
    vout_ref, tout_ref,
    band_ref, mask_ref, k_a, k_b, k_c, v_a, v_b, v_c, vq, tq, tk, tv, vproj, tproj, state_o, state_m, weights_ref, attn, wpair, relay,
    kv_send, kv_recv, sib_recv, relay_recv, load_sem,
    t_a, t_ar, t_b, t_br, t_c, t_cr, t_zr, t_rows, t_sums, t_sumr, t_out,
    ta_sem, tz_sem, tg_sem, ts_sem, to_sem,
    swap_in, keep, y_out, y_in, z_out, z_in,
    w_sem, swap_sem, y_send, y_recv, z_send, z_recv,
):
    frm = lax.axis_index("frm")
    head = lax.axis_index("head")
    zh, x, c = frm // 8, (frm // 2) % 4, frm % 2
    zl, y = head // 4, head % 4
    xr, xo = x // 2, x % 2

    def at(zh_, x_, c_):
        return {"frm": zh_ * 8 + x_ * 2 + c_, "head": head}

    def at_head(zl_, y_):
        return {"frm": frm, "head": zl_ * 4 + y_}

    x_mate = x + 1 - 2 * xo
    sib = at(zh, x, 1 - c)
    mate = at(zh, x_mate, c)
    inter = at(zh, 3 - x, c)
    z_pair = at_head(1 - zl, y)
    y_of = (y + 1 - 2 * (y % 2), 3 - y)
    y_opp = (y + 2) % 4
    y_pair = (at_head(zl, y_of[0]), at_head(zl, y_of[1]))
    zh_to = zh + 1 - 2 * xr
    v_send = (zh_to >= 0) & (zh_to <= 3)
    zh_from = zh - 1 + 2 * xr
    v_recv = (zh_from >= 0) & (zh_from <= 3)
    vert = at(jnp.clip(zh_to, 0, 3), x, c)
    far = at(jnp.clip(zh_from, 0, 3), x, c)

    def copy_to(src, dst, send, recv, device):
        return pltpu.make_async_remote_copy(
            src_ref=src, dst_ref=dst, send_sem=send, recv_sem=recv,
            device_id=device, device_id_type=MESH,
        )

    loads = []

    def load(src, dst):
        copy = pltpu.make_async_copy(src, dst, load_sem.at[len(loads)])
        copy.start()
        loads.append(copy)
        return copy

    load_own = [load(vk_hbm, k_a.at[0]), load(vv_hbm, v_a.at[0])]
    load_text = [
        load(tq_hbm, tq), load(tk_hbm, tk), load(tv_hbm, tv), load(mask_hbm, mask_ref), load(band_hbm, band_ref)
    ]
    load_q = load(vq_hbm, vq)
    load_vproj = load(vproj_hbm, vproj)
    load_tproj = load(tproj_hbm.at[:, pl.ds(pl.multiple_of(x * 768, 768), 768)], tproj)

    frm_partners = [sib]
    frm_partners += [at((zh + d) % 4, x, c) for d in range(1, 4)]
    frm_partners += [at(zh, (x + d) % 4, c) for d in range(1, 4)]
    head_partners = [
        ((zl + dz) % 2, (y + dy) % 4) for dz in range(2) for dy in range(4) if (dz, dy) != (0, 0)
    ]
    barrier = pltpu.get_barrier_semaphore()
    with jax.named_scope("barrier"):
        for device in frm_partners + [at_head(a, b) for a, b in head_partners]:
            pl.semaphore_signal(barrier, inc=1, device_id=device, device_id_type=MESH)
        pl.semaphore_wait(barrier, len(frm_partners) + len(head_partners))

    rows = 256 // CHUNKS
    sends = []

    def kv_copy(kind, t, j, src_slot, dst_slot, device, src=None):
        rng = pl.ds(j * rows, rows)
        return copy_to(
            kv_of[t][src_slot // 4].at[src_slot % 4, rng] if src is None else src.at[rng],
            kv_of[t][dst_slot // 4].at[dst_slot % 4, rng],
            kv_send.at[kind],
            sib_recv.at[dst_slot // 2, t] if dst_slot % 2 else kv_recv.at[dst_slot // 2, t, j],
            device,
        )

    kv_of = ((k_a, k_b, k_c), (v_a, v_b, v_c))
    pieces = [(t, j) for t in range(2) for j in range(CHUNKS)]
    own_hbm = (vk_hbm, vv_hbm)

    def to_mate(t, j):
        return kv_copy(0, t, j, 0, 2 * MATE, mate, own_hbm[t])

    def to_inter(t, j):
        return kv_copy(1, t, j, 0, 2 * INTER, inter, own_hbm[t])

    def to_opp(t, j):
        if (t, j) in OPP_BY_MATE:
            return kv_copy(2, t, j, 2 * INTER, 2 * OPP, mate)
        return kv_copy(2, t, j, 2 * MATE, 2 * OPP, inter)

    def to_far(which, t, j):
        k = FAR.index((t, j))
        rng = pl.ds(j * rows, rows)
        return copy_to(
            own_hbm[t].at[rng] if which == 0 else kv_of[t][0].at[2 * MATE, rng],
            relay.at[which, k], kv_send.at[11 + which], relay_recv.at[which, k], far,
        )

    def to_relayed(which, t, j):
        k = FAR.index((t, j))
        role = (VERT, VMATE)[which]
        return copy_to(
            relay.at[which, k], kv_of[t][2].at[2 * role % 4, pl.ds(j * rows, rows)],
            kv_send.at[13 + which], kv_recv.at[role, t, j], inter,
        )

    def to_vert(t, j):
        return kv_copy(3, t, j, 2 * INTER, 2 * VERT, vert)

    def to_vmate(t, j):
        return kv_copy(4, t, j, 2 * VERT, 2 * VMATE, mate)

    def to_sib(role, t, j):
        return kv_copy(5 + role, t, j, 2 * role, 2 * role + 1, sib, own_hbm[t] if role == OWN else None)

    def go(copy):
        copy.start()
        sends.append(copy)

    def wait_bytes(ref, sem):
        copy_to(ref, ref, sem, kv_recv.at[0, 0, 0], sib).wait_send()

    def send_own(todo_inter, todo_mate):
        for p_inter, p_mate in zip(todo_inter, todo_mate):
            to_inter(*p_inter).start()
            to_mate(*p_mate).start()
            to_sib(OWN, *p_mate).start()

    (k0, k1, k2, k3), (v0, v1, v2, v3) = [[quarter(t, k) for k in range(4)] for t in range(2)]
    order_inter = k0 + k1 + k2 + k3 + v0 + v1 + v2 + v3
    order_mate = k0 + k1 + v2 + v3 + k2 + k3 + v0 + v1
    send_own(order_inter[:CHUNKS], order_mate[:CHUNKS])

    @pl.when(v_recv)
    def _():
        for t, j in FAR:
            to_far(0, t, j).start()

    def to_pair(pair):
        cols = pl.ds(pl.multiple_of(2 * PART * pair + PART * c, PART), PART)
        return copy_to(vproj_hbm.at[:, cols], wpair.at[pair, c], w_sem.at[0], w_sem.at[1 + pair], y_pair[pair])

    def pair_to_sib(pair):
        return copy_to(wpair.at[pair, c], wpair.at[pair, c], w_sem.at[3], w_sem.at[4], sib)

    for pair in range(2):
        to_pair(pair).start()

    for copy in load_own + load_text:
        copy.wait()
    lane = lax.broadcasted_iota(jnp.int32, (1, TXT), 1)
    text_bias = jnp.where(mask_ref[...] == 1, 0.0, DEAD)
    first_bias = jnp.where(frm == 0, text_bias, DEAD)

    def pack_stats(tops, totals):
        count = tops[0].shape[0]
        at_lane = lax.broadcasted_iota(jnp.int32, (count, HD), 1)
        packed = jnp.zeros((count, HD), F32)
        for h in range(HEADS_HERE):
            high = totals[h].astype(BF).astype(F32)
            packed = jnp.where(at_lane == h, tops[h], packed)
            packed = jnp.where(at_lane == 3 + h, high, packed)
            packed = jnp.where(at_lane == 6 + h, totals[h] - high, packed)
        return packed

    def text_partial():
        tops, totals, mixed = [], [], []
        for h in range(HEADS_HERE):
            cols = slice(h * HD, (h + 1) * HD)
            s_own = dot_nt(tq[:, cols], k_a[0, :, cols])
            s_text = dot_nt(tq[:, cols], tk[:, cols]) + first_bias
            top = jnp.maximum(
                jnp.max(s_own, axis=1, keepdims=True), jnp.max(s_text, axis=1, keepdims=True)
            ).astype(BF).astype(F32)
            base = top * FACTOR
            w_own = jnp.exp2(s_own * FACTOR - base).astype(BF)
            w_text = jnp.exp2(s_text * FACTOR - base).astype(BF)
            both = dot_nn(w_own, with_ones(v_a[0, :, cols])) + dot_nn(w_text, with_ones(tv[:, cols]))
            tops.append(top)
            totals.append(both[:, HD:HD + 1])
            mixed.append(both[:, :HD].astype(BF))
        stats = pack_stats(tops, totals).astype(BF)
        for h_to in range(8):
            for half in range(2):
                rng = slice(32 * h_to + 16 * half, 32 * h_to + 16 * half + 16)
                for h in range(HEADS_HERE):
                    t_a[half, h_to, :, h * HD:(h + 1) * HD] = mixed[h][rng]
                t_a[half, h_to, :, LANES:] = stats[rng]

    with jax.named_scope("text_partial"):
        text_partial()
    text_a = copy_to(t_a.at[1 - c], t_ar, ta_sem.at[0], ta_sem.at[1], sib)
    go(text_a)

    def merge(parts):
        parts = [p.astype(F32) for p in parts]
        out_tops, out_totals, out_mixed = [], [], []
        for h in range(HEADS_HERE):
            tops_h = [p[:, LANES + h:LANES + h + 1] for p in parts]
            top = tops_h[0]
            for other in tops_h[1:]:
                top = jnp.maximum(top, other)
            total, mix = 0.0, 0.0
            for p, top_p in zip(parts, tops_h):
                weight = jnp.exp2((top_p - top) * FACTOR)
                total_p = p[:, LANES + 3 + h:LANES + 4 + h] + p[:, LANES + 6 + h:LANES + 7 + h]
                total = total + total_p * weight
                mix = mix + p[:, h * HD:(h + 1) * HD] * weight
            out_tops.append(top)
            out_totals.append(total)
            out_mixed.append(mix)
        return out_tops, out_totals, out_mixed

    def merged(parts):
        out_tops, out_totals, out_mixed = merge(parts)
        return jnp.concatenate(out_mixed + [pack_stats(out_tops, out_totals)], axis=1)

    def slots_of_window():
        mid = c != xo
        pick_same = mid & (band_ref[0] == xo)
        return (0, jnp.where(mid, 3, 1), jnp.where(pick_same, 1, 2))

    def group_scores(g, with_text):
        slots = slots_of_window()
        for h in range(HEADS_HERE):
            cols = slice(h * HD, (h + 1) * HD)
            query = vq[:, cols]
            scores = [dot_nt(query, kv_of[0][g][s, :, cols]) for s in slots]
            if with_text:
                scores.append(dot_nt(query, tk[:, cols]) + text_bias)
            top = scores[0]
            for score in scores[1:]:
                top = jnp.maximum(top, score)
            top = jnp.max(top, axis=1, keepdims=True)
            base = top * FACTOR
            for i, score in enumerate(scores):
                weights_ref[g, h, i] = jnp.exp2(score * FACTOR - base).astype(BF)
            state_m[g, h] = jnp.broadcast_to(top, (256, HD))

    def group_values(g, with_text):
        slots = slots_of_window()
        for h in range(HEADS_HERE):
            cols = slice(h * HD, (h + 1) * HD)
            total = dot_nn(weights_ref[g, h, 0], with_ones(kv_of[1][g][slots[0], :, cols]))
            for i in (1, 2):
                total = total + dot_nn(weights_ref[g, h, i], with_ones(kv_of[1][g][slots[i], :, cols]))
            if with_text:
                total = total + dot_nn(weights_ref[g, h, 3], with_ones(tv[:, cols]))
            state_o[g, h] = total

    def join_groups():
        for h in range(HEADS_HERE):
            tops = [state_m[g, h] for g in range(3)]
            top = jnp.maximum(jnp.maximum(tops[0], tops[1]), tops[2])
            mix, total = 0.0, 0.0
            for g in range(3):
                factor = jnp.exp2((tops[g] - top) * FACTOR)
                mix = mix + state_o[g, h, :, :HD] * factor
                total = total + state_o[g, h, :, HD:] * factor
            attn[:, :, :, h * HD:(h + 1) * HD] = (mix / total).astype(BF).reshape(2, 4, 32, HD)

    def serve_inter(t, j):
        to_inter(t, j).wait_recv()
        to_sib(INTER, t, j).start()
        if (t, j) in OPP_BY_MATE:
            to_opp(t, j).start()

    def serve_mate(t, j):
        to_mate(t, j).wait_recv()
        if (t, j) in FAR:
            @pl.when(v_recv)
            def _():
                to_far(1, t, j).start()

        to_sib(MATE, t, j).start()
        if (t, j) not in OPP_BY_MATE:
            to_opp(t, j).start()

    def pass_own(t, j):
        @pl.when(v_send)
        def _():
            to_far(0, t, j).wait_recv()
            to_relayed(0, t, j).start()

    def pass_mate(t, j):
        @pl.when(v_send)
        def _():
            to_far(1, t, j).wait_recv()
            to_relayed(1, t, j).start()

    def serve_far(t, j):
        @pl.when(v_recv)
        def _():
            to_relayed(0, t, j).wait_recv()
            to_sib(VERT, t, j).start()
            to_relayed(1, t, j).wait_recv()
            to_sib(VMATE, t, j).start()

    def send_vert(t, j):
        @pl.when(v_send)
        def _():
            to_vert(t, j).start()

    def text_step_a():
        text_a.wait_recv()
        for h_to in range(8):
            t_b[h_to // 4, h_to % 4] = merged([t_a[c, h_to], t_ar[h_to]]).astype(BF)
        copy = copy_to(t_b.at[1 - xr], t_br, ta_sem.at[2], ta_sem.at[3], inter)
        go(copy)
        return copy

    def text_step_b(copy):
        copy.wait_recv()
        for k in range(4):
            t_c[k // 2, k % 2] = merged([t_b[xr, k], t_br[k]]).astype(BF)
        copy = copy_to(t_c.at[1 - xo], t_cr, ta_sem.at[4], ta_sem.at[5], mate)
        go(copy)
        return copy

    def text_step_c(copy):
        copy.wait_recv()
        for k in range(2):
            t_zr[zh, k] = merged([t_c[xo, k], t_cr[k]]).astype(BF)
        for dz in range(1, 4):
            copy_to(t_zr.at[zh], t_zr.at[zh], tz_sem.at[0], tz_sem.at[1], at((zh + dz) % 4, x, c)).start()

    def text_step_z():
        block = t_zr.at[pl.ds(1, 3)]
        copy_to(block, block, tz_sem.at[0], tz_sem.at[1], sib).wait_recv()
        for k in range(2):
            _, sums, mix = merge([t_zr[i, k] for i in range(4)])
            for h in range(HEADS_HERE):
                t_rows[x, k, :, h * HD:(h + 1) * HD] = (mix[h] / sums[h]).astype(BF)
        for dx in range(1, 4):
            copy_to(t_rows.at[x], t_rows.at[x], tg_sem.at[0], tg_sem.at[1], at(zh, (x + dx) % 4, c)).start()

    def text_gather():
        block = t_rows.at[pl.ds(0, 3)]
        copy_to(block, block, tg_sem.at[0], tg_sem.at[1], sib).wait_recv()
        load_tproj.wait()
        rows_all = t_rows[...].reshape(128, LANES)
        product = dot_nn(rows_all, tproj[...]).astype(BF)
        for k in range(8):
            t_sums[k] = product[16 * k:16 * k + 16]
        for k, (a, b) in enumerate(head_partners):
            copy_to(t_sums.at[a * 4 + b], t_sumr.at[k], ts_sem.at[0], ts_sem.at[1], at_head(a, b)).start()

    def text_sum():
        copy_to(t_sumr, t_sumr, ts_sem.at[0], ts_sem.at[1], sib).wait_recv()
        total = t_sums[head].astype(F32)
        for k in range(7):
            total = total + t_sumr[k].astype(F32)
        t_out[c, x] = total.astype(BF)
        for dx in range(1, 4):
            block = t_out.at[c, x]
            copy_to(block, block, to_sem.at[0], to_sem.at[1], at(zh, (x + dx) % 4, c)).start()

    def text_spread_sib():
        block = t_out.at[c, pl.ds(0, 3)]
        copy_to(block, block, to_sem.at[0], to_sem.at[1], sib).wait_recv()
        go(copy_to(t_out.at[c], t_out.at[c], to_sem.at[2], to_sem.at[3], sib))

    def text_finish():
        block = t_out.at[1 - c]
        copy_to(block, block, to_sem.at[2], to_sem.at[3], sib).wait_recv()
        for cc in range(2):
            for k in range(4):
                tout_ref[16 * cc:16 * cc + 16, k * 768:(k + 1) * 768] = t_out[cc, k].astype(F32)

    def serve_vert(t, j):
        @pl.when(v_recv)
        def _():
            to_vert(t, j).wait_recv()
            to_vmate(t, j).start()
            to_sib(VERT, t, j).start()

    def serve_vmate(t, j):
        @pl.when(v_recv)
        def _():
            to_vmate(t, j).wait_recv()
            to_sib(VMATE, t, j).start()

    def wait_sib(roles, t):
        for role in roles:
            block = kv_of[t][(2 * role + 1) // 4].at[(2 * role + 1) % 4]
            copy_to(block, block, kv_send.at[0], sib_recv.at[role, t], sib).wait_recv()

    def wait_sib_vert(t):
        @pl.when(v_recv)
        def _():
            wait_sib((VERT, VMATE), t)

    def serve_opp(t, j):
        to_opp(t, j).wait_recv()
        to_sib(OPP, t, j).start()

    scope = jax.named_scope
    def many(step, todo):
        with scope(step.__name__):
            for p in todo:
                step(*p)

    def part_of(todo, lo, hi):
        return todo[lo * CHUNKS // 4:hi * CHUNKS // 4]

    def first_hop(lo, hi):
        for k in range(lo * PER, hi * PER):
            many(serve_inter, [order_inter[k]])
            if order_inter[k] not in FAR:
                many(send_vert, [order_inter[k]])
            many(serve_mate, [order_mate[k]])

    with scope("text_sibling_merge"):
        text_copy = text_step_a()
        send_own(order_inter[CHUNKS:], order_mate[CHUNKS:])
    first_hop(0, 4)
    with scope("text_inter_merge"):
        text_copy = text_step_b(text_copy)
    first_hop(4, 6)
    many(pass_own, FAR)
    with scope("text_mate_merge"):
        text_step_c(text_copy)
    first_hop(6, 8)
    many(pass_mate, FAR)
    many(serve_vert, k0 + k1)
    many(serve_vert, k2)
    many(serve_opp, k0 + k1)
    many(serve_vert, k3)
    with scope("wait_own_frame"):
        load_q.wait()
        wait_sib((OWN, MATE), 0)
        wait_sib((OWN, MATE), 1)
    with scope("own_frame"):
        group_scores(0, True)
        group_values(0, True)
    many(serve_vert, v0)
    many(serve_opp, k2 + k3)
    many(serve_vmate, k0 + k1 + k2)
    with scope("projection_halves"):
        for pair in range(2):
            to_pair(pair).wait_recv()
            pair_to_sib(pair).start()
    many(serve_vert, v1)
    with scope("text_z_merge"):
        text_step_z()
    with scope("wait_beside_keys"):
        wait_sib((OPP, INTER), 0)
    with scope("frame_beside_scores"):
        group_scores(1, False)
    many(serve_vmate, k3)
    many(serve_opp, v0 + v1 + v2 + v3)
    many(serve_far, FAR)
    many(serve_vmate, v0 + v1)
    with scope("text_gather"):
        text_gather()
    with scope("wait_across_keys"):
        wait_sib_vert(0)
    with scope("frame_across_scores"):
        @pl.when(v_recv)
        def _():
            group_scores(2, False)

        @pl.when(jnp.logical_not(v_recv))
        def _():
            state_m[2] = jnp.full((HEADS_HERE, 256, HD), DEAD, F32)
            state_o[2] = jnp.zeros((HEADS_HERE, 256, 2 * HD), F32)
    with scope("wait_beside_values"):
        wait_sib((OPP, INTER), 1)
    with scope("frame_beside_values"):
        group_values(1, False)
    with scope("wait_across_values"):
        wait_sib_vert(1)
    with scope("frame_across_values"):
        @pl.when(v_recv)
        def _():
            group_values(2, False)
    with scope("join_groups"):
        join_groups()
    swap_own, swap_pair = [attn.at[:, y_of[0]], attn.at[:, y_of[1]]], attn.at[:, y_opp]
    for pair in range(2):
        copy_to(swap_own[pair], swap_in.at[pair, 0], swap_sem.at[0], swap_sem.at[1 + pair], y_pair[pair]).start()
        copy_to(swap_pair, swap_in.at[pair, 1], swap_sem.at[0], swap_sem.at[1 + pair], y_pair[pair]).start()

    def own_rows(pair):
        return jnp.concatenate(
            [attn[:, y].reshape(64, LANES), attn[:, y_of[1 - pair]].reshape(64, LANES)], axis=0
        )

    with scope("project_own"):
        load_vproj.wait()
        for pair in range(2):
            rows_here = own_rows(pair)
            for q in range(2):
                lo = (2 * pair + q) * PART
                product = dot_nn(rows_here, vproj[:, lo:lo + PART])
                keep[pair, 2 * q], keep[pair, 2 * q + 1] = product[:, :HALF], product[:, HALF:]
        copy_to(wpair.at[0], wpair.at[0], w_sem.at[3], w_sem.at[4], sib).wait_recv()
    parts_of = [(pair, q) for q in range(4) for pair in range(2)]
    for pair in range(2):
        with scope("swap_wait"):
            copy_to(swap_in.at[pair], swap_in.at[pair], swap_sem.at[0], swap_sem.at[1 + pair], sib).wait_recv()
    for pair, q in parts_of:
        if q % 2 == 0:
            with scope("project_pair"):
                product = dot_nn(swap_in[pair].reshape(128, LANES), wpair[pair, q // 2])
                for k in range(2):
                    total = keep[pair, q + k] + product[:, k * HALF:(k + 1) * HALF]
                    y_out[pair, q + k] = total[64:].astype(BF)
                    keep[pair, q + k, :64] = total[:64]
                    copy_to(
                        y_out.at[pair, q + k], y_in.at[pair, q + k], y_send.at[0], y_recv.at[pair, q + k],
                        y_pair[1 - pair],
                    ).start()
    with scope("text_sum"):
        text_sum()
    for pair, q in parts_of:
        with scope("y_wait"):
            came = y_in.at[pair, q]
            copy_to(came, came, y_send.at[0], y_recv.at[pair, q], sib).wait_recv()
        with scope("y_sum"):
            lo = (4 * pair + q) * HALF
            total = keep[pair, q, :64] + y_in[pair, q].astype(F32)
            vout_ref[:, lo:lo + HALF] = jnp.where(zl == 0, total[:32], total[32:])
            z_out[pair, q] = jnp.where(zl == 0, total[32:], total[:32]).astype(BF)
        copy_to(z_out.at[pair, q], z_in.at[pair, q], z_send.at[0], z_recv.at[pair, q], z_pair).start()
    with scope("text_spread_sib"):
        text_spread_sib()
    for pair, q in parts_of:
        with scope("z_wait"):
            came = z_in.at[pair, q]
            copy_to(came, came, z_send.at[0], z_recv.at[pair, q], sib).wait_recv()
        lo = (4 * pair + q) * HALF
        vout_ref[:, lo:lo + HALF] = vout_ref[:, lo:lo + HALF] + z_in[pair, q].astype(F32)

    with scope("text_finish"):
        text_finish()
    with scope("wait_sends"):
        for copy in sends:
            copy.wait_send()

        whole = k_a.at[pl.ds(0, 2)]
        for kind in (0, 1, 2, 5 + OWN, 5 + MATE, 5 + OPP, 5 + INTER):
            wait_bytes(whole, kv_send.at[kind])

        most, fourth = k_a.at[pl.ds(0, 3), pl.ds(0, 128)], k_a.at[0, pl.ds(0, 128)]

        @pl.when(v_send)
        def _():
            wait_bytes(most, kv_send.at[3])
            wait_bytes(fourth, kv_send.at[13])
            wait_bytes(fourth, kv_send.at[14])

        @pl.when(v_recv)
        def _():
            wait_bytes(most, kv_send.at[4])
            wait_bytes(whole, kv_send.at[5 + VERT])
            wait_bytes(whole, kv_send.at[5 + VMATE])
            wait_bytes(fourth, kv_send.at[11])
            wait_bytes(fourth, kv_send.at[12])

        wait_bytes(t_zr.at[pl.ds(1, 3)], tz_sem.at[0])
        wait_bytes(t_rows.at[pl.ds(0, 3)], tg_sem.at[0])
        wait_bytes(t_sumr, ts_sem.at[0])
        wait_bytes(t_out.at[0, pl.ds(0, 3)], to_sem.at[0])
        wait_bytes(wpair.at[0], w_sem.at[0])
        wait_bytes(wpair.at[0], w_sem.at[3])
        wait_bytes(swap_in, swap_sem.at[0])
        wait_bytes(y_in, y_send.at[0])
        wait_bytes(z_in, z_send.at[0])


def store(video, text, video_out, text_out, sems):
    copies = [
        pltpu.make_async_copy(video, video_out, sems.at[0]),
        pltpu.make_async_copy(text, text_out, sems.at[1]),
    ]
    for copy in copies:
        copy.start()
    for copy in copies:
        copy.wait()


def body(video_q, video_k, video_v, text_q, text_k, text_v, band_start, text_mask, video_proj, text_proj):
    dma = pltpu.SemaphoreType.DMA
    vmem = pltpu.VMEM
    hbm_spec = pl.BlockSpec(memory_space=pltpu.HBM)
    vmem_spec = pl.BlockSpec(memory_space=pltpu.VMEM)
    outs = pl.pallas_call(
        kernel,
        name="joint_attention",
        out_shape=(pltpu.VMEM((32, WIDTH), F32), pltpu.VMEM((32, WIDTH), F32)),
        in_specs=[hbm_spec] * 10,
        out_specs=(vmem_spec, vmem_spec),
        scratch_shapes=[
            pltpu.SMEM((1,), jnp.int32),
            vmem((1, TXT), jnp.int32),
            *[vmem((4, 256, LANES), BF) for _ in range(6)],
            vmem((256, LANES), BF),
            vmem((256, LANES), BF),
            vmem((256, LANES), BF),
            vmem((256, LANES), BF),
            vmem((LANES, WIDTH), BF),
            vmem((LANES, 768), BF),
            vmem((3, HEADS_HERE, 256, 2 * HD), F32),
            vmem((3, HEADS_HERE, 256, HD), F32),
            vmem((3, HEADS_HERE, 4, 256, 256), BF),
            vmem((2, 4, 32, LANES), BF),
            vmem((2, 2, LANES, PART), BF),
            vmem((2, len(FAR), 256 // CHUNKS, LANES), BF),
            dma((15,)),
            dma((6, 2, CHUNKS)),
            dma((6, 2)),
            dma((2, len(FAR))),
            dma((10,)),
            vmem((2, 8, 16, 512), BF),
            vmem((8, 16, 512), BF),
            vmem((2, 4, 16, 512), BF),
            vmem((4, 16, 512), BF),
            vmem((2, 2, 16, 512), BF),
            vmem((2, 16, 512), BF),
            vmem((4, 2, 16, 512), BF),
            vmem((4, 2, 16, LANES), BF),
            vmem((8, 16, 768), BF),
            vmem((7, 16, 768), BF),
            vmem((2, 4, 16, 768), BF),
            dma((6,)),
            dma((2,)),
            dma((2,)),
            dma((2,)),
            dma((4,)),
            vmem((2, 2, 2, 32, LANES), BF),
            vmem((2, 4, 128, HALF), F32),
            vmem((2, 4, 64, HALF), BF),
            vmem((2, 4, 64, HALF), BF),
            vmem((2, 4, 32, HALF), BF),
            vmem((2, 4, 32, HALF), BF),
            dma((5,)),
            dma((3,)),
            dma((1,)),
            dma((2, 4)),
            dma((1,)),
            dma((2, 4)),
        ],
        compiler_params=pltpu.CompilerParams(
            collective_id=0, has_side_effects=True, vmem_limit_bytes=56 * 2**20
        ),
        cost_estimate=pl.CostEstimate(flops=2_000_000_000, bytes_accessed=8_000_000, transcendentals=2_500_000),
    )(
        video_q, video_k, video_v, text_q, text_k, text_v, band_start, text_mask.reshape(1, TXT),
        video_proj, text_proj,
    )
    result = jax.ShapeDtypeStruct((32, WIDTH), F32)
    return pl.pallas_call(
        store,
        name="store",
        out_shape=(result, result),
        in_specs=[vmem_spec, vmem_spec],
        out_specs=(hbm_spec, hbm_spec),
        scratch_shapes=[dma((2,))],
    )(*[pltpu.with_memory_space_constraint(out, pltpu.VMEM) for out in outs])


def solution(mesh):
    return jax.shard_map(
        body,
        mesh=mesh,
        in_specs=(
            P("frm", "head"), P("frm", "head"), P("frm", "head"),
            P(None, "head"), P(None, "head"), P(None, "head"),
            P("frm"), P(), P("head", None), P("head", None),
        ),
        out_specs=(P(("frm", "head"), None), P("head", None)),
        check_vma=False,
    )
```

```python
import math

import jax
import jax.numpy as jnp
from jax import lax
from jax.experimental import pallas as pl
from jax.experimental.pallas import tpu as pltpu
from jax.sharding import PartitionSpec as P

HD = 128
TXT = 256
BANDS = 4
HEADS_HERE = 3
LANES = HEADS_HERE * HD
WIDTH = 3072
MESH = pl.DeviceIdType.MESH
BF = jnp.bfloat16
F32 = jnp.float32
FACTOR = math.log2(math.e) / math.sqrt(HD)
DEAD = -1e30
CHUNKS = 4
OWN, MATE, OPP, INTER, VMATE, VERT = range(6)
PER = CHUNKS // 4


def quarter(t, k):
    return tuple((t, k * PER + i) for i in range(PER))


FAR = quarter(1, 2) + quarter(1, 3)
OPP_BY_MATE = quarter(1, 0) + quarter(1, 1) + quarter(1, 2)
PART = 768
HALF = PART // 2


def dot_nt(a, b):
    return lax.dot_general(a, b, (((1,), (1,)), ((), ())), preferred_element_type=F32)


def dot_nn(a, b):
    return jnp.dot(a, b, preferred_element_type=F32)


def with_ones(values):
    return jnp.concatenate([values, jnp.ones(values.shape, BF)], axis=1)


def kernel(
    vq_hbm, vk_hbm, vv_hbm, tq_hbm, tk_hbm, tv_hbm, band_hbm, mask_hbm, vproj_hbm, tproj_hbm,
    vout_ref, tout_ref,
    band_ref, mask_ref, k_a, k_b, k_c, v_a, v_b, v_c, vq, tq, tk, tv, vproj, tproj, state_o, state_m, weights_ref, attn, wpair, relay,
    kv_send, kv_recv, sib_recv, relay_recv, load_sem,
    t_a, t_ar, t_b, t_br, t_c, t_cr, t_zr, t_rows, t_sums, t_sumr, t_out,
    ta_sem, tz_sem, tg_sem, ts_sem, to_sem,
    swap_in, keep, y_out, y_in, z_out, z_in,
    w_sem, swap_sem, y_send, y_recv, z_send, z_recv,
):
    frm = lax.axis_index("frm")
    head = lax.axis_index("head")
    zh, x, c = frm // 8, (frm // 2) % 4, frm % 2
    zl, y = head // 4, head % 4
    xr, xo = x // 2, x % 2

    def at(zh_, x_, c_):
        return {"frm": zh_ * 8 + x_ * 2 + c_, "head": head}

    def at_head(zl_, y_):
        return {"frm": frm, "head": zl_ * 4 + y_}

    x_mate = x + 1 - 2 * xo
    sib = at(zh, x, 1 - c)
    mate = at(zh, x_mate, c)
    inter = at(zh, 3 - x, c)
    z_pair = at_head(1 - zl, y)
    y_of = (y + 1 - 2 * (y % 2), 3 - y)
    y_opp = (y + 2) % 4
    y_pair = (at_head(zl, y_of[0]), at_head(zl, y_of[1]))
    zh_to = zh + 1 - 2 * xr
    v_send = (zh_to >= 0) & (zh_to <= 3)
    zh_from = zh - 1 + 2 * xr
    v_recv = (zh_from >= 0) & (zh_from <= 3)
    vert = at(jnp.clip(zh_to, 0, 3), x, c)
    far = at(jnp.clip(zh_from, 0, 3), x, c)

    def copy_to(src, dst, send, recv, device):
        return pltpu.make_async_remote_copy(
            src_ref=src, dst_ref=dst, send_sem=send, recv_sem=recv,
            device_id=device, device_id_type=MESH,
        )

    loads = []

    def load(src, dst):
        copy = pltpu.make_async_copy(src, dst, load_sem.at[len(loads)])
        copy.start()
        loads.append(copy)
        return copy

    load_own = [load(vk_hbm, k_a.at[0]), load(vv_hbm, v_a.at[0])]
    load_text = [
        load(tq_hbm, tq), load(tk_hbm, tk), load(tv_hbm, tv), load(mask_hbm, mask_ref), load(band_hbm, band_ref)
    ]
    load_q = load(vq_hbm, vq)
    load_vproj = load(vproj_hbm, vproj)
    load_tproj = load(tproj_hbm.at[:, pl.ds(pl.multiple_of(x * 768, 768), 768)], tproj)

    frm_partners = [sib]
    frm_partners += [at((zh + d) % 4, x, c) for d in range(1, 4)]
    frm_partners += [at(zh, (x + d) % 4, c) for d in range(1, 4)]
    head_partners = [
        ((zl + dz) % 2, (y + dy) % 4) for dz in range(2) for dy in range(4) if (dz, dy) != (0, 0)
    ]
    barrier = pltpu.get_barrier_semaphore()
    with jax.named_scope("barrier"):
        for device in frm_partners + [at_head(a, b) for a, b in head_partners]:
            pl.semaphore_signal(barrier, inc=1, device_id=device, device_id_type=MESH)
        pl.semaphore_wait(barrier, len(frm_partners) + len(head_partners))

    rows = 256 // CHUNKS
    sends = []

    def kv_copy(kind, t, j, src_slot, dst_slot, device, src=None):
        rng = pl.ds(j * rows, rows)
        return copy_to(
            kv_of[t][src_slot // 4].at[src_slot % 4, rng] if src is None else src.at[rng],
            kv_of[t][dst_slot // 4].at[dst_slot % 4, rng],
            kv_send.at[kind],
            sib_recv.at[dst_slot // 2, t] if dst_slot % 2 else kv_recv.at[dst_slot // 2, t, j],
            device,
        )

    kv_of = ((k_a, k_b, k_c), (v_a, v_b, v_c))
    pieces = [(t, j) for t in range(2) for j in range(CHUNKS)]
    own_hbm = (vk_hbm, vv_hbm)

    def to_mate(t, j):
        return kv_copy(0, t, j, 0, 2 * MATE, mate, own_hbm[t])

    def to_inter(t, j):
        return kv_copy(1, t, j, 0, 2 * INTER, inter, own_hbm[t])

    def to_opp(t, j):
        if (t, j) in OPP_BY_MATE:
            return kv_copy(2, t, j, 2 * INTER, 2 * OPP, mate)
        return kv_copy(2, t, j, 2 * MATE, 2 * OPP, inter)

    def to_far(which, t, j):
        k = FAR.index((t, j))
        rng = pl.ds(j * rows, rows)
        return copy_to(
            own_hbm[t].at[rng] if which == 0 else kv_of[t][0].at[2 * MATE, rng],
            relay.at[which, k], kv_send.at[11 + which], relay_recv.at[which, k], far,
        )

    def to_relayed(which, t, j):
        k = FAR.index((t, j))
        role = (VERT, VMATE)[which]
        return copy_to(
            relay.at[which, k], kv_of[t][2].at[2 * role % 4, pl.ds(j * rows, rows)],
            kv_send.at[13 + which], kv_recv.at[role, t, j], inter,
        )

    def to_vert(t, j):
        return kv_copy(3, t, j, 2 * INTER, 2 * VERT, vert)

    def to_vmate(t, j):
        return kv_copy(4, t, j, 2 * VERT, 2 * VMATE, mate)

    def to_sib(role, t, j):
        return kv_copy(5 + role, t, j, 2 * role, 2 * role + 1, sib, own_hbm[t] if role == OWN else None)

    def go(copy):
        copy.start()
        sends.append(copy)

    def wait_bytes(ref, sem):
        copy_to(ref, ref, sem, kv_recv.at[0, 0, 0], sib).wait_send()

    def send_own(todo_inter, todo_mate):
        for p_inter, p_mate in zip(todo_inter, todo_mate):
            to_inter(*p_inter).start()
            to_mate(*p_mate).start()
            to_sib(OWN, *p_mate).start()

    (k0, k1, k2, k3), (v0, v1, v2, v3) = [[quarter(t, k) for k in range(4)] for t in range(2)]
    order_inter = k0 + k1 + k2 + k3 + v0 + v1 + v2 + v3
    order_mate = k0 + k1 + v2 + v3 + k2 + k3 + v0 + v1
    send_own(order_inter[:CHUNKS], order_mate[:CHUNKS])

    @pl.when(v_recv)
    def _():
        for t, j in FAR:
            to_far(0, t, j).start()

    def to_pair(pair):
        cols = pl.ds(pl.multiple_of(2 * PART * pair + PART * c, PART), PART)
        return copy_to(vproj_hbm.at[:, cols], wpair.at[pair, c], w_sem.at[0], w_sem.at[1 + pair], y_pair[pair])

    def pair_to_sib(pair):
        return copy_to(wpair.at[pair, c], wpair.at[pair, c], w_sem.at[3], w_sem.at[4], sib)

    for pair in range(2):
        to_pair(pair).start()

    for copy in load_own + load_text:
        copy.wait()
    lane = lax.broadcasted_iota(jnp.int32, (1, TXT), 1)
    text_bias = jnp.where(mask_ref[...] == 1, 0.0, DEAD)
    first_bias = jnp.where(frm == 0, text_bias, DEAD)

    def pack_stats(tops, totals):
        count = tops[0].shape[0]
        at_lane = lax.broadcasted_iota(jnp.int32, (count, HD), 1)
        packed = jnp.zeros((count, HD), F32)
        for h in range(HEADS_HERE):
            high = totals[h].astype(BF).astype(F32)
            packed = jnp.where(at_lane == h, tops[h], packed)
            packed = jnp.where(at_lane == 3 + h, high, packed)
            packed = jnp.where(at_lane == 6 + h, totals[h] - high, packed)
        return packed

    def text_partial():
        tops, totals, mixed = [], [], []
        for h in range(HEADS_HERE):
            cols = slice(h * HD, (h + 1) * HD)
            s_own = dot_nt(tq[:, cols], k_a[0, :, cols])
            s_text = dot_nt(tq[:, cols], tk[:, cols]) + first_bias
            top = jnp.maximum(
                jnp.max(s_own, axis=1, keepdims=True), jnp.max(s_text, axis=1, keepdims=True)
            ).astype(BF).astype(F32)
            base = top * FACTOR
            w_own = jnp.exp2(s_own * FACTOR - base).astype(BF)
            w_text = jnp.exp2(s_text * FACTOR - base).astype(BF)
            both = dot_nn(w_own, with_ones(v_a[0, :, cols])) + dot_nn(w_text, with_ones(tv[:, cols]))
            tops.append(top)
            totals.append(both[:, HD:HD + 1])
            mixed.append(both[:, :HD].astype(BF))
        stats = pack_stats(tops, totals).astype(BF)
        for h_to in range(8):
            for half in range(2):
                rng = slice(32 * h_to + 16 * half, 32 * h_to + 16 * half + 16)
                for h in range(HEADS_HERE):
                    t_a[half, h_to, :, h * HD:(h + 1) * HD] = mixed[h][rng]
                t_a[half, h_to, :, LANES:] = stats[rng]

    with jax.named_scope("text_partial"):
        text_partial()
    text_a = copy_to(t_a.at[1 - c], t_ar, ta_sem.at[0], ta_sem.at[1], sib)
    go(text_a)

    def merge(parts):
        parts = [p.astype(F32) for p in parts]
        out_tops, out_totals, out_mixed = [], [], []
        for h in range(HEADS_HERE):
            tops_h = [p[:, LANES + h:LANES + h + 1] for p in parts]
            top = tops_h[0]
            for other in tops_h[1:]:
                top = jnp.maximum(top, other)
            total, mix = 0.0, 0.0
            for p, top_p in zip(parts, tops_h):
                weight = jnp.exp2((top_p - top) * FACTOR)
                total_p = p[:, LANES + 3 + h:LANES + 4 + h] + p[:, LANES + 6 + h:LANES + 7 + h]
                total = total + total_p * weight
                mix = mix + p[:, h * HD:(h + 1) * HD] * weight
            out_tops.append(top)
            out_totals.append(total)
            out_mixed.append(mix)
        return out_tops, out_totals, out_mixed

    def merged(parts):
        out_tops, out_totals, out_mixed = merge(parts)
        return jnp.concatenate(out_mixed + [pack_stats(out_tops, out_totals)], axis=1)

    def slots_of_window():
        mid = c != xo
        pick_same = mid & (band_ref[0] == xo)
        return (0, jnp.where(mid, 3, 1), jnp.where(pick_same, 1, 2))

    def group_scores(g, with_text):
        slots = slots_of_window()
        for h in range(HEADS_HERE):
            cols = slice(h * HD, (h + 1) * HD)
            query = vq[:, cols]
            scores = [dot_nt(query, kv_of[0][g][s, :, cols]) for s in slots]
            if with_text:
                scores.append(dot_nt(query, tk[:, cols]) + text_bias)
            top = scores[0]
            for score in scores[1:]:
                top = jnp.maximum(top, score)
            top = jnp.max(top, axis=1, keepdims=True)
            base = top * FACTOR
            for i, score in enumerate(scores):
                weights_ref[g, h, i] = jnp.exp2(score * FACTOR - base).astype(BF)
            state_m[g, h] = jnp.broadcast_to(top, (256, HD))

    def group_values(g, with_text):
        slots = slots_of_window()
        for h in range(HEADS_HERE):
            cols = slice(h * HD, (h + 1) * HD)
            total = dot_nn(weights_ref[g, h, 0], with_ones(kv_of[1][g][slots[0], :, cols]))
            for i in (1, 2):
                total = total + dot_nn(weights_ref[g, h, i], with_ones(kv_of[1][g][slots[i], :, cols]))
            if with_text:
                total = total + dot_nn(weights_ref[g, h, 3], with_ones(tv[:, cols]))
            state_o[g, h] = total

    def join_groups():
        for h in range(HEADS_HERE):
            tops = [state_m[g, h] for g in range(3)]
            top = jnp.maximum(jnp.maximum(tops[0], tops[1]), tops[2])
            mix, total = 0.0, 0.0
            for g in range(3):
                factor = jnp.exp2((tops[g] - top) * FACTOR)
                mix = mix + state_o[g, h, :, :HD] * factor
                total = total + state_o[g, h, :, HD:] * factor
            attn[:, :, :, h * HD:(h + 1) * HD] = (mix / total).astype(BF).reshape(2, 4, 32, HD)

    def serve_inter(t, j):
        to_inter(t, j).wait_recv()
        to_sib(INTER, t, j).start()
        if (t, j) in OPP_BY_MATE:
            to_opp(t, j).start()

    def serve_mate(t, j):
        to_mate(t, j).wait_recv()
        if (t, j) in FAR:
            @pl.when(v_recv)
            def _():
                to_far(1, t, j).start()

        to_sib(MATE, t, j).start()
        if (t, j) not in OPP_BY_MATE:
            to_opp(t, j).start()

    def pass_own(t, j):
        @pl.when(v_send)
        def _():
            to_far(0, t, j).wait_recv()
            to_relayed(0, t, j).start()

    def pass_mate(t, j):
        @pl.when(v_send)
        def _():
            to_far(1, t, j).wait_recv()
            to_relayed(1, t, j).start()

    def serve_far(t, j):
        @pl.when(v_recv)
        def _():
            to_relayed(0, t, j).wait_recv()
            to_sib(VERT, t, j).start()
            to_relayed(1, t, j).wait_recv()
            to_sib(VMATE, t, j).start()

    def send_vert(t, j):
        @pl.when(v_send)
        def _():
            to_vert(t, j).start()

    def text_step_a():
        text_a.wait_recv()
        for h_to in range(8):
            t_b[h_to // 4, h_to % 4] = merged([t_a[c, h_to], t_ar[h_to]]).astype(BF)
        copy = copy_to(t_b.at[1 - xr], t_br, ta_sem.at[2], ta_sem.at[3], inter)
        go(copy)
        return copy

    def text_step_b(copy):
        copy.wait_recv()
        for k in range(4):
            t_c[k // 2, k % 2] = merged([t_b[xr, k], t_br[k]]).astype(BF)
        copy = copy_to(t_c.at[1 - xo], t_cr, ta_sem.at[4], ta_sem.at[5], mate)
        go(copy)
        return copy

    def text_step_c(copy):
        copy.wait_recv()
        for k in range(2):
            t_zr[zh, k] = merged([t_c[xo, k], t_cr[k]]).astype(BF)
        for dz in range(1, 4):
            copy_to(t_zr.at[zh], t_zr.at[zh], tz_sem.at[0], tz_sem.at[1], at((zh + dz) % 4, x, c)).start()

    def text_step_z():
        block = t_zr.at[pl.ds(1, 3)]
        copy_to(block, block, tz_sem.at[0], tz_sem.at[1], sib).wait_recv()
        for k in range(2):
            _, sums, mix = merge([t_zr[i, k] for i in range(4)])
            for h in range(HEADS_HERE):
                t_rows[x, k, :, h * HD:(h + 1) * HD] = (mix[h] / sums[h]).astype(BF)
        for dx in range(1, 4):
            copy_to(t_rows.at[x], t_rows.at[x], tg_sem.at[0], tg_sem.at[1], at(zh, (x + dx) % 4, c)).start()

    def text_gather():
        block = t_rows.at[pl.ds(0, 3)]
        copy_to(block, block, tg_sem.at[0], tg_sem.at[1], sib).wait_recv()
        load_tproj.wait()
        rows_all = t_rows[...].reshape(128, LANES)
        product = dot_nn(rows_all, tproj[...]).astype(BF)
        for k in range(8):
            t_sums[k] = product[16 * k:16 * k + 16]
        for k, (a, b) in enumerate(head_partners):
            copy_to(t_sums.at[a * 4 + b], t_sumr.at[k], ts_sem.at[0], ts_sem.at[1], at_head(a, b)).start()

    def text_sum():
        copy_to(t_sumr, t_sumr, ts_sem.at[0], ts_sem.at[1], sib).wait_recv()
        total = t_sums[head].astype(F32)
        for k in range(7):
            total = total + t_sumr[k].astype(F32)
        t_out[c, x] = total.astype(BF)
        for dx in range(1, 4):
            block = t_out.at[c, x]
            copy_to(block, block, to_sem.at[0], to_sem.at[1], at(zh, (x + dx) % 4, c)).start()

    def text_spread_sib():
        block = t_out.at[c, pl.ds(0, 3)]
        copy_to(block, block, to_sem.at[0], to_sem.at[1], sib).wait_recv()
        go(copy_to(t_out.at[c], t_out.at[c], to_sem.at[2], to_sem.at[3], sib))

    def text_finish():
        block = t_out.at[1 - c]
        copy_to(block, block, to_sem.at[2], to_sem.at[3], sib).wait_recv()
        for cc in range(2):
            for k in range(4):
                tout_ref[16 * cc:16 * cc + 16, k * 768:(k + 1) * 768] = t_out[cc, k].astype(F32)

    def serve_vert(t, j):
        @pl.when(v_recv)
        def _():
            to_vert(t, j).wait_recv()
            to_vmate(t, j).start()
            to_sib(VERT, t, j).start()

    def serve_vmate(t, j):
        @pl.when(v_recv)
        def _():
            to_vmate(t, j).wait_recv()
            to_sib(VMATE, t, j).start()

    def wait_sib(roles, t):
        for role in roles:
            block = kv_of[t][(2 * role + 1) // 4].at[(2 * role + 1) % 4]
            copy_to(block, block, kv_send.at[0], sib_recv.at[role, t], sib).wait_recv()

    def wait_sib_vert(t):
        @pl.when(v_recv)
        def _():
            wait_sib((VERT, VMATE), t)

    def serve_opp(t, j):
        to_opp(t, j).wait_recv()
        to_sib(OPP, t, j).start()

    scope = jax.named_scope
    def many(step, todo):
        with scope(step.__name__):
            for p in todo:
                step(*p)

    def part_of(todo, lo, hi):
        return todo[lo * CHUNKS // 4:hi * CHUNKS // 4]

    def first_hop(lo, hi):
        for k in range(lo * PER, hi * PER):
            many(serve_inter, [order_inter[k]])
            if order_inter[k] not in FAR:
                many(send_vert, [order_inter[k]])
            many(serve_mate, [order_mate[k]])

    with scope("text_sibling_merge"):
        text_copy = text_step_a()
        send_own(order_inter[CHUNKS:], order_mate[CHUNKS:])
    first_hop(0, 4)
    with scope("text_inter_merge"):
        text_copy = text_step_b(text_copy)
    first_hop(4, 6)
    many(pass_own, FAR)
    with scope("text_mate_merge"):
        text_step_c(text_copy)
    first_hop(6, 8)
    many(pass_mate, FAR)
    many(serve_vert, k0 + k1)
    many(serve_vert, k2)
    many(serve_opp, k0 + k1)
    many(serve_vert, k3)
    with scope("wait_own_frame"):
        load_q.wait()
        wait_sib((OWN, MATE), 0)
        wait_sib((OWN, MATE), 1)
    with scope("own_frame"):
        group_scores(0, True)
        group_values(0, True)
    many(serve_vert, v0)
    many(serve_opp, k2 + k3)
    many(serve_vmate, k0 + k1 + k2)
    with scope("projection_halves"):
        for pair in range(2):
            to_pair(pair).wait_recv()
            pair_to_sib(pair).start()
    many(serve_vert, v1)
    with scope("text_z_merge"):
        text_step_z()
    with scope("wait_beside_keys"):
        wait_sib((OPP, INTER), 0)
    with scope("frame_beside_scores"):
        group_scores(1, False)
    many(serve_vmate, k3)
    many(serve_opp, v0 + v1 + v2 + v3)
    many(serve_far, FAR)
    many(serve_vmate, v0 + v1)
    with scope("text_gather"):
        text_gather()
    with scope("wait_across_keys"):
        wait_sib_vert(0)
    with scope("frame_across_scores"):
        @pl.when(v_recv)
        def _():
            group_scores(2, False)

        @pl.when(jnp.logical_not(v_recv))
        def _():
            state_m[2] = jnp.full((HEADS_HERE, 256, HD), DEAD, F32)
            state_o[2] = jnp.zeros((HEADS_HERE, 256, 2 * HD), F32)
    with scope("wait_beside_values"):
        wait_sib((OPP, INTER), 1)
    with scope("frame_beside_values"):
        group_values(1, False)
    with scope("wait_across_values"):
        wait_sib_vert(1)
    with scope("frame_across_values"):
        @pl.when(v_recv)
        def _():
            group_values(2, False)
    with scope("join_groups"):
        join_groups()
    swap_own, swap_pair = [attn.at[:, y_of[0]], attn.at[:, y_of[1]]], attn.at[:, y_opp]
    for pair in range(2):
        copy_to(swap_own[pair], swap_in.at[pair, 0], swap_sem.at[0], swap_sem.at[1 + pair], y_pair[pair]).start()
        copy_to(swap_pair, swap_in.at[pair, 1], swap_sem.at[0], swap_sem.at[1 + pair], y_pair[pair]).start()

    def own_rows(pair):
        return jnp.concatenate(
            [attn[:, y].reshape(64, LANES), attn[:, y_of[1 - pair]].reshape(64, LANES)], axis=0
        )

    with scope("project_own"):
        load_vproj.wait()
        for pair in range(2):
            rows_here = own_rows(pair)
            for q in range(2):
                lo = (2 * pair + q) * PART
                product = dot_nn(rows_here, vproj[:, lo:lo + PART])
                keep[pair, 2 * q], keep[pair, 2 * q + 1] = product[:, :HALF], product[:, HALF:]
        copy_to(wpair.at[0], wpair.at[0], w_sem.at[3], w_sem.at[4], sib).wait_recv()
    with scope("text_sum"):
        text_sum()
    parts_of = [(pair, q) for q in range(4) for pair in range(2)]
    for pair in range(2):
        with scope("swap_wait"):
            copy_to(swap_in.at[pair], swap_in.at[pair], swap_sem.at[0], swap_sem.at[1 + pair], sib).wait_recv()
    for pair, q in parts_of:
        if q % 2 == 0:
            with scope("project_pair"):
                product = dot_nn(swap_in[pair].reshape(128, LANES), wpair[pair, q // 2])
                for k in range(2):
                    total = keep[pair, q + k] + product[:, k * HALF:(k + 1) * HALF]
                    y_out[pair, q + k] = total[64:].astype(BF)
                    keep[pair, q + k, :64] = total[:64]
                    copy_to(
                        y_out.at[pair, q + k], y_in.at[pair, q + k], y_send.at[0], y_recv.at[pair, q + k],
                        y_pair[1 - pair],
                    ).start()
    for pair, q in parts_of:
        with scope("y_wait"):
            came = y_in.at[pair, q]
            copy_to(came, came, y_send.at[0], y_recv.at[pair, q], sib).wait_recv()
        with scope("y_sum"):
            lo = (4 * pair + q) * HALF
            total = keep[pair, q, :64] + y_in[pair, q].astype(F32)
            vout_ref[:, lo:lo + HALF] = jnp.where(zl == 0, total[:32], total[32:])
            z_out[pair, q] = jnp.where(zl == 0, total[32:], total[:32]).astype(BF)
        copy_to(z_out.at[pair, q], z_in.at[pair, q], z_send.at[0], z_recv.at[pair, q], z_pair).start()
    with scope("text_spread_sib"):
        text_spread_sib()
    for pair, q in parts_of:
        with scope("z_wait"):
            came = z_in.at[pair, q]
            copy_to(came, came, z_send.at[0], z_recv.at[pair, q], sib).wait_recv()
        lo = (4 * pair + q) * HALF
        vout_ref[:, lo:lo + HALF] = vout_ref[:, lo:lo + HALF] + z_in[pair, q].astype(F32)

    with scope("text_finish"):
        text_finish()
    with scope("wait_sends"):
        for copy in sends:
            copy.wait_send()

        whole = k_a.at[pl.ds(0, 2)]
        for kind in (0, 1, 2, 5 + OWN, 5 + MATE, 5 + OPP, 5 + INTER):
            wait_bytes(whole, kv_send.at[kind])

        most, fourth = k_a.at[pl.ds(0, 3), pl.ds(0, 128)], k_a.at[0, pl.ds(0, 128)]

        @pl.when(v_send)
        def _():
            wait_bytes(most, kv_send.at[3])
            wait_bytes(fourth, kv_send.at[13])
            wait_bytes(fourth, kv_send.at[14])

        @pl.when(v_recv)
        def _():
            wait_bytes(most, kv_send.at[4])
            wait_bytes(whole, kv_send.at[5 + VERT])
            wait_bytes(whole, kv_send.at[5 + VMATE])
            wait_bytes(fourth, kv_send.at[11])
            wait_bytes(fourth, kv_send.at[12])

        wait_bytes(t_zr.at[pl.ds(1, 3)], tz_sem.at[0])
        wait_bytes(t_rows.at[pl.ds(0, 3)], tg_sem.at[0])
        wait_bytes(t_sumr, ts_sem.at[0])
        wait_bytes(t_out.at[0, pl.ds(0, 3)], to_sem.at[0])
        wait_bytes(wpair.at[0], w_sem.at[0])
        wait_bytes(wpair.at[0], w_sem.at[3])
        wait_bytes(swap_in, swap_sem.at[0])
        wait_bytes(y_in, y_send.at[0])
        wait_bytes(z_in, z_send.at[0])


def store(video, text, video_out, text_out, sems):
    copies = [
        pltpu.make_async_copy(video, video_out, sems.at[0]),
        pltpu.make_async_copy(text, text_out, sems.at[1]),
    ]
    for copy in copies:
        copy.start()
    for copy in copies:
        copy.wait()


def body(video_q, video_k, video_v, text_q, text_k, text_v, band_start, text_mask, video_proj, text_proj):
    dma = pltpu.SemaphoreType.DMA
    vmem = pltpu.VMEM
    hbm_spec = pl.BlockSpec(memory_space=pltpu.HBM)
    vmem_spec = pl.BlockSpec(memory_space=pltpu.VMEM)
    outs = pl.pallas_call(
        kernel,
        name="joint_attention",
        out_shape=(pltpu.VMEM((32, WIDTH), F32), pltpu.VMEM((32, WIDTH), F32)),
        in_specs=[hbm_spec] * 10,
        out_specs=(vmem_spec, vmem_spec),
        scratch_shapes=[
            pltpu.SMEM((1,), jnp.int32),
            vmem((1, TXT), jnp.int32),
            *[vmem((4, 256, LANES), BF) for _ in range(6)],
            vmem((256, LANES), BF),
            vmem((256, LANES), BF),
            vmem((256, LANES), BF),
            vmem((256, LANES), BF),
            vmem((LANES, WIDTH), BF),
            vmem((LANES, 768), BF),
            vmem((3, HEADS_HERE, 256, 2 * HD), F32),
            vmem((3, HEADS_HERE, 256, HD), F32),
            vmem((3, HEADS_HERE, 4, 256, 256), BF),
            vmem((2, 4, 32, LANES), BF),
            vmem((2, 2, LANES, PART), BF),
            vmem((2, len(FAR), 256 // CHUNKS, LANES), BF),
            dma((15,)),
            dma((6, 2, CHUNKS)),
            dma((6, 2)),
            dma((2, len(FAR))),
            dma((10,)),
            vmem((2, 8, 16, 512), BF),
            vmem((8, 16, 512), BF),
            vmem((2, 4, 16, 512), BF),
            vmem((4, 16, 512), BF),
            vmem((2, 2, 16, 512), BF),
            vmem((2, 16, 512), BF),
            vmem((4, 2, 16, 512), BF),
            vmem((4, 2, 16, LANES), BF),
            vmem((8, 16, 768), BF),
            vmem((7, 16, 768), BF),
            vmem((2, 4, 16, 768), BF),
            dma((6,)),
            dma((2,)),
            dma((2,)),
            dma((2,)),
            dma((4,)),
            vmem((2, 2, 2, 32, LANES), BF),
            vmem((2, 4, 128, HALF), F32),
            vmem((2, 4, 64, HALF), BF),
            vmem((2, 4, 64, HALF), BF),
            vmem((2, 4, 32, HALF), BF),
            vmem((2, 4, 32, HALF), BF),
            dma((5,)),
            dma((3,)),
            dma((1,)),
            dma((2, 4)),
            dma((1,)),
            dma((2, 4)),
        ],
        compiler_params=pltpu.CompilerParams(
            collective_id=0, has_side_effects=True, vmem_limit_bytes=56 * 2**20
        ),
        cost_estimate=pl.CostEstimate(flops=2_000_000_000, bytes_accessed=8_000_000, transcendentals=2_500_000),
    )(
        video_q, video_k, video_v, text_q, text_k, text_v, band_start, text_mask.reshape(1, TXT),
        video_proj, text_proj,
    )
    result = jax.ShapeDtypeStruct((32, WIDTH), F32)
    return pl.pallas_call(
        store,
        name="store",
        out_shape=(result, result),
        in_specs=[vmem_spec, vmem_spec],
        out_specs=(hbm_spec, hbm_spec),
        scratch_shapes=[dma((2,))],
    )(*[pltpu.with_memory_space_constraint(out, pltpu.VMEM) for out in outs])


def solution(mesh):
    return jax.shard_map(
        body,
        mesh=mesh,
        in_specs=(
            P("frm", "head"), P("frm", "head"), P("frm", "head"),
            P(None, "head"), P(None, "head"), P(None, "head"),
            P("frm"), P(), P("head", None), P("head", None),
        ),
        out_specs=(P(("frm", "head"), None), P("head", None)),
        check_vma=False,
    )
```
